32 devices in a mesh: band: 8 (over z, y), feat: 4 (over x, core).
Axes of the slice: x: 2, y: 2, z: 4, core: 2. Of those that a mesh axis runs over, the one named last changes fastest.
Arguments:
- grid_latent: bfloat16 [2048, 512], P('band', 'feat'), may hold values from -6 to 6
- mesh_latent: bfloat16 [2048, 512], P('band', 'feat'), may hold values from -6 to 6
- w_grid: bfloat16 [512, 512], P(None, 'feat'), may hold values from -0.25 to 0.25
- w_mesh: bfloat16 [512, 512], P(None, 'feat'), may hold values from -0.25 to 0.25
- w_enc_out: bfloat16 [512, 512], P('feat'), may hold values from -0.25 to 0.25
- w_send: bfloat16 [512, 512], P(None, 'feat'), may hold values from -0.25 to 0.25
- w_recv: bfloat16 [512, 512], P(None, 'feat'), may hold values from -0.25 to 0.25
- w_proc_out: bfloat16 [512, 512], P('feat'), may hold values from -0.25 to 0.25
- grid_send: int32 [64, 64], P('band'), may hold values from 0 to 255
- g2m_src: int32 [64, 128], P('band'), may hold values from 0 to 511
- g2m_dst: int32 [64, 128], P('band'), may hold values from 0 to 255
- mesh_send: int32 [64, 32], P('band'), may hold values from 0 to 255
- m2m_src: int32 [64, 128], P('band'), may hold values from 0 to 511
- m2m_dst: int32 [64, 128], P('band'), may hold values from 0 to 255
- cotangent: bfloat16 [2048, 512], P('band', 'feat'), may hold values from -6 to 6
Outputs:
- mesh_out: bfloat16 [2048, 512], P('band', 'feat')
- grid_grad: bfloat16 [2048, 512], P('band', 'feat')
- grad_w_grid: float32 [512, 512], P(None, 'feat')
- grad_w_mesh: float32 [512, 512], P(None, 'feat')
- grad_w_enc_out: float32 [512, 512], P('feat')
- grad_w_send: float32 [512, 512], P(None, 'feat')
- grad_w_recv: float32 [512, 512], P(None, 'feat')
- grad_w_proc_out: float32 [512, 512], P('feat')
The draws below stay inside these ranges and needn't reach their ends.
Inputs may be any that keep to these rules, and one draw needn't show every extreme that they name: `grid_send`: local grid row indices of the sending band. `mesh_send`: local mesh row indices of the sending partition. `m2m_src`: values under 256 are own rows, the rest halo slots.
All inputs are finite; a program needn't handle non-finite values.
Results may differ from the reference program's by a relative error of at most 0.014.
Values may be sent and summed in bfloat16 or wider, within the bound.
A program may use at most 64 MiB of HBM per device.

```python
import math
import jax
import jax.numpy as jnp
import numpy as np
from jax import lax

LATENT = 512
HIDDEN_SIZE = 512
GRID_DEV = 256
MESH_DEV = 256
ENC_EDGES = 1024
PROC_EDGES = 1024
SLOTS_DEV = 512
HALO_DEV = 256
GRID_PEER = 64
HALO_PEER = 32
GRID_ROWS = 2048
MESH_ROWS = 2048
N_BAND = 8


def place_ends(entries, own_key, smallest, top_value):
    extent = entries.shape
    spot = [jax.random.randint(jax.random.fold_in(own_key, axis), (), 0, extent[axis]) for axis in range(len(extent))]
    entries = entries.at[tuple(spot)].set(smallest)
    longest = extent.index(max(extent))
    spot[longest] = (spot[longest] + 1) % extent[longest]
    return entries.at[tuple(spot)].set(top_value)


def levels(stream_key, shape, pieces, low, top_value):
    def one(position, parts):
        heights = jax.random.uniform(jax.random.fold_in(jax.random.fold_in(stream_key, 6), position), (parts,), jnp.float32, low / len(pieces), top_value / len(pieces))
        return jnp.repeat(jnp.exp(heights), shape[position] // parts).reshape((-1,) + (1,) * (len(shape) - position - 1))

    loudness = one(*pieces[0])
    for cut in pieces[1:]:
        loudness = loudness * one(*cut)
    return loudness


def rank_table(count, skew):
    loads = [(1 << 20) // math.isqrt(rank ** skew) + 1 for rank in range(1, count + 1)]
    width = 1 + sum(loads) // (1 << 30)
    return np.cumsum(np.array([max(1, weight // width) for weight in loads]))


def ranked(key, extent, number_of, slope):
    grid = rank_table(number_of, slope)
    pick = jax.random.randint(jax.random.fold_in(key, 1), extent, 0, int(grid[number_of - 1]))
    standing = jnp.searchsorted(jnp.asarray(grid, jnp.int32), pick, side="right")
    return jax.random.permutation(jax.random.fold_in(key, 2), number_of)[standing].astype(jnp.int32)


def normal_values(stream_key, extent, spread, bound, shards=(), kind=jnp.bfloat16):
    factor_of = levels(stream_key, extent, shards, -0.22, 0.18) if shards else 1.0
    values = jax.random.normal(stream_key, extent, jnp.float32) * spread * factor_of
    return jnp.minimum(jnp.maximum(values, -bound), bound).astype(kind)


def setup_inputs(seed: int = 0) -> dict:
    splits = jax.random.split(jax.random.key(seed), 16)
    grid_latent = normal_values(splits[0], (GRID_ROWS, LATENT), 1.0, 6.0, ((0, 8), (1, 4)))
    mesh_latent = normal_values(splits[1], (MESH_ROWS, LATENT), 1.0, 6.0, ((0, 8), (1, 4)))
    w_grid = normal_values(splits[2], (LATENT, HIDDEN_SIZE), LATENT ** -0.5, 0.25, ((1, 4),))
    w_mesh = normal_values(splits[3], (LATENT, HIDDEN_SIZE), LATENT ** -0.5, 0.25, ((1, 4),))
    w_enc_out = normal_values(splits[4], (HIDDEN_SIZE, LATENT), HIDDEN_SIZE ** -0.5, 0.25, ((0, 4),))
    w_send = normal_values(splits[5], (LATENT, HIDDEN_SIZE), LATENT ** -0.5, 0.25, ((1, 4),))
    w_recv = normal_values(splits[6], (LATENT, HIDDEN_SIZE), LATENT ** -0.5, 0.25, ((1, 4),))
    w_proc_out = normal_values(splits[7], (HIDDEN_SIZE, LATENT), HIDDEN_SIZE ** -0.5, 0.25, ((0, 4),))
    grid_send = place_ends(jax.random.randint(splits[8], (N_BAND * N_BAND, GRID_PEER), 0, GRID_DEV), jax.random.fold_in(splits[8], 1), 0, GRID_DEV - 1).astype(jnp.int32)
    g2m_src = place_ends(jax.random.randint(splits[9], (N_BAND * ENC_EDGES // 128, 128), 0, SLOTS_DEV), jax.random.fold_in(splits[9], 1), 0, SLOTS_DEV - 1).astype(jnp.int32)
    g2m_dst = place_ends(ranked(splits[10], (N_BAND * ENC_EDGES // 128, 128), MESH_DEV, 1), jax.random.fold_in(splits[10], 3), 0, MESH_DEV - 1).astype(jnp.int32)
    mesh_send = place_ends(jax.random.randint(splits[11], (N_BAND * N_BAND, HALO_PEER), 0, MESH_DEV), jax.random.fold_in(splits[11], 1), 0, MESH_DEV - 1).astype(jnp.int32)
    m2m_src = place_ends(jax.random.randint(splits[12], (N_BAND * PROC_EDGES // 128, 128), 0, MESH_DEV + HALO_DEV), jax.random.fold_in(splits[12], 1), 0, (MESH_DEV + HALO_DEV) - 1).astype(jnp.int32)
    m2m_dst = place_ends(jax.random.randint(splits[13], (N_BAND * PROC_EDGES // 128, 128), 0, MESH_DEV), jax.random.fold_in(splits[13], 1), 0, MESH_DEV - 1).astype(jnp.int32)
    cotangent = normal_values(splits[14], (MESH_ROWS, LATENT), 1.0, 6.0, ((0, 8), (1, 4)))
    return {"grid_latent": grid_latent, "mesh_latent": mesh_latent, "w_grid": w_grid, "w_mesh": w_mesh, "w_enc_out": w_enc_out, "w_send": w_send, "w_recv": w_recv, "w_proc_out": w_proc_out, "grid_send": grid_send, "g2m_src": g2m_src, "g2m_dst": g2m_dst, "mesh_send": mesh_send, "m2m_src": m2m_src, "m2m_dst": m2m_dst, "cotangent": cotangent}


def silu_slope(values):
    sigma = jax.nn.sigmoid(values)
    return sigma * (1.0 + values * (1.0 - sigma))

def matmul(left, right):
    return jnp.dot(left, right, preferred_element_type=jnp.float32)

def inner_rows(left, right):
    return lax.dot_general(left, right, (((0,), (0,)), ((), ())), preferred_element_type=jnp.float32)

def reference(grid_latent, mesh_latent, w_grid, w_mesh, w_enc_out, w_send, w_recv, w_proc_out, grid_send, g2m_src, g2m_dst, mesh_send, m2m_src, m2m_dst, cotangent):
    band_ids = jnp.arange(N_BAND, dtype=jnp.int32)
    slot_row = (grid_send.reshape(N_BAND, N_BAND, GRID_PEER) + (band_ids * GRID_DEV)[:, None, None]).transpose(1, 0, 2).reshape(N_BAND, SLOTS_DEV)
    enc_slot = g2m_src.reshape(N_BAND, ENC_EDGES)
    enc_source = jnp.take_along_axis(slot_row, enc_slot, axis=1).reshape(-1)
    enc_target = (g2m_dst.reshape(N_BAND, ENC_EDGES) + (band_ids * MESH_DEV)[:, None]).reshape(-1)
    halo_row = (mesh_send.reshape(N_BAND, N_BAND, HALO_PEER) + (band_ids * MESH_DEV)[:, None, None]).transpose(1, 0, 2).reshape(N_BAND, HALO_DEV)
    local_row = band_ids[:, None] * MESH_DEV + jnp.arange(MESH_DEV, dtype=jnp.int32)[None, :]
    ext_row = jnp.concatenate([local_row, halo_row], axis=1)
    proc_slot = m2m_src.reshape(N_BAND, PROC_EDGES)
    proc_source = jnp.take_along_axis(ext_row, proc_slot, axis=1).reshape(-1)
    proc_target = (m2m_dst.reshape(N_BAND, PROC_EDGES) + (band_ids * MESH_DEV)[:, None]).reshape(-1)
    proj_grid = matmul(grid_latent, w_grid).astype(jnp.bfloat16)
    proj_mesh = matmul(mesh_latent, w_mesh).astype(jnp.bfloat16)
    enc_pre = jnp.take(proj_grid, enc_source, axis=0).astype(jnp.float32) + jnp.take(proj_mesh, enc_target, axis=0).astype(jnp.float32)
    enc_active = jax.nn.silu(enc_pre).astype(jnp.bfloat16)
    enc_summed = jax.ops.segment_sum(enc_active.astype(jnp.float32), enc_target, num_segments=MESH_ROWS).astype(jnp.bfloat16)
    mesh_mid = (mesh_latent.astype(jnp.float32) + matmul(enc_summed, w_enc_out)).astype(jnp.bfloat16)
    proj_send = matmul(mesh_mid, w_send).astype(jnp.bfloat16)
    proj_recv = matmul(mesh_mid, w_recv).astype(jnp.bfloat16)
    proc_pre = jnp.take(proj_send, proc_source, axis=0).astype(jnp.float32) + jnp.take(proj_recv, proc_target, axis=0).astype(jnp.float32)
    proc_active = jax.nn.silu(proc_pre).astype(jnp.bfloat16)
    proc_summed = jax.ops.segment_sum(proc_active.astype(jnp.float32), proc_target, num_segments=MESH_ROWS).astype(jnp.bfloat16)
    mesh_out = (mesh_mid.astype(jnp.float32) + matmul(proc_summed, w_proc_out)).astype(jnp.bfloat16)
    scale = 1.0 / math.sqrt(MESH_ROWS)
    back_proc = matmul(cotangent, w_proc_out.T).astype(jnp.bfloat16)
    grad_w_proc_out = inner_rows(proc_summed, cotangent) * scale
    slope_proc = (jnp.take(back_proc, proc_target, axis=0).astype(jnp.float32) * silu_slope(proc_pre)).astype(jnp.bfloat16)
    back_recv = jax.ops.segment_sum(slope_proc.astype(jnp.float32), proc_target, num_segments=MESH_ROWS).astype(jnp.bfloat16)
    ext_ids = (proc_slot + (band_ids * (MESH_DEV + HALO_DEV))[:, None]).reshape(-1)
    back_ext = jax.ops.segment_sum(slope_proc.astype(jnp.float32), ext_ids, num_segments=N_BAND * (MESH_DEV + HALO_DEV)).astype(jnp.bfloat16)
    back_send = jax.ops.segment_sum(back_ext.astype(jnp.float32), ext_row.reshape(-1), num_segments=MESH_ROWS).astype(jnp.bfloat16)
    grad_w_send = inner_rows(mesh_mid, back_send) * scale
    grad_w_recv = inner_rows(mesh_mid, back_recv) * scale
    back_mid = (cotangent.astype(jnp.float32) + matmul(back_send, w_send.T) + matmul(back_recv, w_recv.T)).astype(jnp.bfloat16)
    back_enc = matmul(back_mid, w_enc_out.T).astype(jnp.bfloat16)
    grad_w_enc_out = inner_rows(enc_summed, back_mid) * scale
    slope_enc = (jnp.take(back_enc, enc_target, axis=0).astype(jnp.float32) * silu_slope(enc_pre)).astype(jnp.bfloat16)
    back_pmesh = jax.ops.segment_sum(slope_enc.astype(jnp.float32), enc_target, num_segments=MESH_ROWS).astype(jnp.bfloat16)
    grad_w_mesh = inner_rows(mesh_latent, back_pmesh) * scale
    slot_ids = (enc_slot + (band_ids * SLOTS_DEV)[:, None]).reshape(-1)
    back_slot = jax.ops.segment_sum(slope_enc.astype(jnp.float32), slot_ids, num_segments=N_BAND * SLOTS_DEV).astype(jnp.bfloat16)
    back_pgrid = jax.ops.segment_sum(back_slot.astype(jnp.float32), slot_row.reshape(-1), num_segments=GRID_ROWS).astype(jnp.bfloat16)
    grad_w_grid = inner_rows(grid_latent, back_pgrid) * scale
    grid_grad = matmul(back_pgrid, w_grid.T).astype(jnp.bfloat16)
    return (mesh_out, grid_grad, grad_w_grid, grad_w_mesh, grad_w_enc_out, grad_w_send, grad_w_recv, grad_w_proc_out)
```

```python
import functools
import math

import jax
import jax.numpy as jnp
from jax import lax
from jax.experimental import pallas as pl
from jax.experimental.pallas import tpu as pltpu
from jax.sharding import PartitionSpec as P


def silu_slope(values):
    sigma = jax.nn.sigmoid(values)
    return sigma * (1.0 + values * (1.0 - sigma))


def matmul(left, right):
    return jnp.dot(left, right, preferred_element_type=jnp.float32)


def inner_rows(left, right):
    return lax.dot_general(
        left, right, (((0,), (0,)), ((), ())), preferred_element_type=jnp.float32
    )


def hot_table(index, count):
    return (index[:, None] == lax.iota(jnp.int32, count)[None, :]).astype(jnp.bfloat16)


def per_device_collectives(
    grid_latent,
    mesh_latent,
    w_grid,
    w_mesh,
    w_enc_out,
    w_send,
    w_recv,
    w_proc_out,
    grid_send,
    g2m_src,
    g2m_dst,
    mesh_send,
    m2m_src,
    m2m_dst,
    cotangent,
):
    bands = lax.axis_size("band")
    grid_rows = grid_latent.shape[0]
    mesh_rows = mesh_latent.shape[0]
    hidden_dev = w_grid.shape[1]
    halo_rows = bands * mesh_send.shape[1]
    slot_rows = bands * grid_send.shape[1]
    scale = 1.0 / math.sqrt(mesh_rows * bands)
    enc_source = g2m_src.reshape(-1)
    enc_target = g2m_dst.reshape(-1)
    proc_source = m2m_src.reshape(-1)
    proc_target = m2m_dst.reshape(-1)
    enc_columns, proc_columns = (
        lax.all_to_all(w_enc_out, "feat", split_axis=1, concat_axis=0, tiled=True),
        lax.all_to_all(w_proc_out, "feat", split_axis=1, concat_axis=0, tiled=True),
    )
    send_slice, recv_slice, grid_slice = (
        lax.all_to_all(w_send, "feat", split_axis=0, concat_axis=1, tiled=True),
        lax.all_to_all(w_recv, "feat", split_axis=0, concat_axis=1, tiled=True),
        lax.all_to_all(w_grid, "feat", split_axis=0, concat_axis=1, tiled=True),
    )
    grid_full = lax.all_gather(grid_latent, "feat", axis=1, tiled=True)
    mesh_full = lax.all_gather(mesh_latent, "feat", axis=1, tiled=True)
    proj_grid = matmul(grid_full, w_grid).astype(jnp.bfloat16)
    outgoing = jnp.take(proj_grid, grid_send, axis=0)
    arrived = lax.all_to_all(outgoing, "band", split_axis=0, concat_axis=0, tiled=True)
    slot_proj = arrived.reshape(slot_rows, hidden_dev)
    proj_mesh = matmul(mesh_full, w_mesh).astype(jnp.bfloat16)
    enc_pre = jnp.take(slot_proj, enc_source, axis=0).astype(jnp.float32) + jnp.take(
        proj_mesh, enc_target, axis=0
    ).astype(jnp.float32)
    enc_active = jax.nn.silu(enc_pre).astype(jnp.bfloat16)
    enc_table = hot_table(enc_target, mesh_rows)
    enc_summed = inner_rows(enc_table, enc_active).astype(jnp.bfloat16)
    enc_whole = lax.all_gather(enc_summed, "feat", axis=1, tiled=True)
    update = matmul(enc_whole, enc_columns)
    mesh_mid = (mesh_latent.astype(jnp.float32) + update).astype(jnp.bfloat16)
    mid_full = lax.all_gather(mesh_mid, "feat", axis=1, tiled=True)
    proj_send = matmul(mid_full, w_send).astype(jnp.bfloat16)
    proj_recv = matmul(mid_full, w_recv).astype(jnp.bfloat16)
    halo_out = jnp.take(proj_send, mesh_send, axis=0)
    halo_in = lax.all_to_all(halo_out, "band", split_axis=0, concat_axis=0, tiled=True)
    extended = jnp.concatenate([proj_send, halo_in.reshape(halo_rows, hidden_dev)], axis=0)
    proc_pre = jnp.take(extended, proc_source, axis=0).astype(jnp.float32) + jnp.take(
        proj_recv, proc_target, axis=0
    ).astype(jnp.float32)
    proc_active = jax.nn.silu(proc_pre).astype(jnp.bfloat16)
    proc_table = hot_table(proc_target, mesh_rows)
    proc_summed = inner_rows(proc_table, proc_active).astype(jnp.bfloat16)
    proc_whole = lax.all_gather(proc_summed, "feat", axis=1, tiled=True)
    proc_update = matmul(proc_whole, proc_columns)
    mesh_out = (mesh_mid.astype(jnp.float32) + proc_update).astype(jnp.bfloat16)
    cot_full = lax.all_gather(cotangent, "feat", axis=1, tiled=True)
    back_proc = matmul(cot_full, w_proc_out.T).astype(jnp.bfloat16)
    grad_proc_out = inner_rows(proc_summed, cot_full)
    slope_proc = (
        jnp.take(back_proc, proc_target, axis=0).astype(jnp.float32) * silu_slope(proc_pre)
    ).astype(jnp.bfloat16)
    back_recv = inner_rows(proc_table, slope_proc).astype(jnp.bfloat16)
    source_table = hot_table(proc_source, mesh_rows + halo_rows)
    back_ext = inner_rows(source_table, slope_proc).astype(jnp.bfloat16)
    back_halo = back_ext[mesh_rows:].reshape(bands, halo_rows // bands, hidden_dev)
    returned = lax.all_to_all(back_halo, "band", split_axis=0, concat_axis=0, tiled=True)
    returned_sum = jax.ops.segment_sum(
        returned.reshape(halo_rows, hidden_dev).astype(jnp.float32),
        mesh_send.reshape(-1),
        num_segments=mesh_rows,
    )
    back_send = (back_ext[:mesh_rows].astype(jnp.float32) + returned_sum).astype(jnp.bfloat16)
    grad_send = inner_rows(mid_full, back_send)
    grad_recv = inner_rows(mid_full, back_recv)
    send_whole, recv_whole = (
        lax.all_gather(back_send, "feat", axis=1, tiled=True),
        lax.all_gather(back_recv, "feat", axis=1, tiled=True),
    )
    back_sum = matmul(send_whole, send_slice.T) + matmul(recv_whole, recv_slice.T)
    back_mid = (cotangent.astype(jnp.float32) + back_sum).astype(jnp.bfloat16)
    back_full = lax.all_gather(back_mid, "feat", axis=1, tiled=True)
    back_enc = matmul(back_full, w_enc_out.T).astype(jnp.bfloat16)
    grad_enc_out = inner_rows(enc_summed, back_full)
    slope_enc = (
        jnp.take(back_enc, enc_target, axis=0).astype(jnp.float32) * silu_slope(enc_pre)
    ).astype(jnp.bfloat16)
    back_pmesh = inner_rows(enc_table, slope_enc).astype(jnp.bfloat16)
    grad_mesh_w = inner_rows(mesh_full, back_pmesh)
    slot_table = hot_table(enc_source, slot_rows)
    back_slot = inner_rows(slot_table, slope_enc).astype(jnp.bfloat16)
    back_slots = lax.all_to_all(
        back_slot.reshape(bands, slot_rows // bands, hidden_dev),
        "band",
        split_axis=0,
        concat_axis=0,
        tiled=True,
    )
    back_pgrid = jax.ops.segment_sum(
        back_slots.reshape(slot_rows, hidden_dev).astype(jnp.float32),
        grid_send.reshape(-1),
        num_segments=grid_rows,
    ).astype(jnp.bfloat16)
    grad_grid_w = inner_rows(grid_full, back_pgrid)
    pgrid_whole = lax.all_gather(back_pgrid, "feat", axis=1, tiled=True)
    grid_grad = matmul(pgrid_whole, grid_slice.T).astype(jnp.bfloat16)
    grad_grid_w, grad_mesh_w, grad_enc_out, grad_send, grad_recv, grad_proc_out = lax.psum(
        (grad_grid_w, grad_mesh_w, grad_enc_out, grad_send, grad_recv, grad_proc_out), "band"
    )
    return (
        mesh_out,
        grid_grad,
        grad_grid_w * scale,
        grad_mesh_w * scale,
        grad_enc_out * scale,
        grad_send * scale,
        grad_recv * scale,
        grad_proc_out * scale,
    )


def inner_columns(left, right):
    return lax.dot_general(
        left, right, (((1,), (1,)), ((), ())), preferred_element_type=jnp.float32
    )


def hot(condition):
    return jnp.where(condition, 1.0, 0.0).astype(jnp.bfloat16)


def sigmoid(values):
    return 1.0 / (1.0 + jnp.exp(-values))


def fused_kernel(
    bands,
    feats,
    scale,
    grid_latent,
    mesh_latent,
    w_grid,
    w_mesh,
    w_enc_out,
    w_send,
    w_recv,
    w_proc_out,
    grid_send,
    g2m_src,
    g2m_dst,
    mesh_send,
    m2m_src,
    m2m_dst,
    cotangent,
    mesh_out,
    grid_grad,
    out_grid,
    out_mesh,
    out_enc,
    out_send,
    out_recv,
    out_proc,
    index_rows,
    index_columns,
    grid_full,
    mesh_full,
    cot_full,
    enc_full,
    send_full,
    recv_full,
    proc_columns,
    grid_slice,
    grid_pick,
    mesh_pick,
    enc_gather,
    enc_scatter,
    proc_gather,
    proc_scatter,
    enc_rows,
    proc_rows,
    outgoing,
    halo_out,
    enc_pre,
    back_edge,
    edge_values,
    edge_slopes,
    enc_whole,
    mid_full,
    proc_whole,
    recv_whole,
    send_whole,
    back_full,
    back_ext,
    halo_back,
    back_slot,
    slot_back,
    pgrid_whole,
    tall_part,
    tall_land,
    tall_sum,
    wide_part,
    wide_land,
    wide_sum,
    feat_send_sem,
    feat_recv_sem,
    band_send_sem,
    band_recv_sem,
):
    band = lax.axis_index("band")
    feat = lax.axis_index("feat")
    width = grid_latent.shape[1]
    rows = mesh_latent.shape[0]
    grid_rows = grid_latent.shape[0]
    slot_peer = grid_send.shape[1]
    halo_peer = mesh_send.shape[1]
    slots = bands * slot_peer
    halos = bands * halo_peer
    edge_rows = g2m_src.shape[0]
    lanes = g2m_src.shape[1]
    ext = rows + halos
    started = []

    def column(place):
        return pl.ds(pl.multiple_of(place * width, width), width)

    def block(place, size):
        return pl.ds(pl.multiple_of(place * size, size), size)

    barrier = pltpu.get_barrier_semaphore()
    for step in range(1, bands):
        pl.semaphore_signal(
            barrier,
            inc=1,
            device_id={"band": lax.rem(band + step, bands)},
            device_id_type=pl.DeviceIdType.MESH,
        )
    for step in range(1, feats):
        pl.semaphore_signal(
            barrier,
            inc=1,
            device_id={"feat": lax.rem(feat + step, feats)},
            device_id_type=pl.DeviceIdType.MESH,
        )
    pl.semaphore_wait(barrier, bands + feats - 2)

    counts = {"feat": 0, "band": 0}

    def exchange(axis, source, target):
        me, size, send_sem, recv_sem = (
            (feat, feats, feat_send_sem, feat_recv_sem)
            if axis == "feat"
            else (band, bands, band_send_sem, band_recv_sem)
        )
        phase = counts[axis]
        counts[axis] += 1
        copies = []
        for step in range(1, size):
            peer = lax.rem(me + step, size)
            copy = pltpu.make_async_remote_copy(
                src_ref=source(peer),
                dst_ref=target(me),
                send_sem=send_sem.at[phase, step - 1],
                recv_sem=recv_sem.at[phase, step - 1],
                device_id={axis: peer},
                device_id_type=pl.DeviceIdType.MESH,
            )
            copy.start()
            copies.append(copy)
        started.extend(copies)
        return copies

    def arrive(copies):
        for copy in copies:
            copy.wait_recv()

    def gather_columns(source, target):
        copies = exchange("feat", lambda peer: source, lambda me: target.at[:, column(me)])
        target[:, column(feat)] = source[...]
        return copies

    def gather_held(target):
        mine = target.at[:, column(feat)]
        return exchange("feat", lambda peer: mine, lambda me: mine)

    grid_copies = gather_columns(grid_latent, grid_full)
    mesh_copies = gather_columns(mesh_latent, mesh_full)

    index_rows[...] = jnp.zeros_like(index_rows)
    index_rows[0:edge_rows, :] = g2m_src[...]
    index_rows[edge_rows : 2 * edge_rows, :] = g2m_dst[...]
    index_rows[2 * edge_rows : 3 * edge_rows, :] = m2m_src[...]
    index_rows[3 * edge_rows : 4 * edge_rows, :] = m2m_dst[...]
    index_rows[4 * edge_rows : 4 * edge_rows + bands, 0:slot_peer] = grid_send[...]
    index_rows[4 * edge_rows + bands : 4 * edge_rows + 2 * bands, 0:halo_peer] = mesh_send[...]
    index_columns[...] = index_rows[...].T

    def picks(target, first, size, count):
        place = lax.broadcasted_iota(jnp.int32, (size, count), 1)
        for peer in range(bands):
            chosen = index_columns[0:size, first + peer : first + peer + 1]
            target[peer * size : (peer + 1) * size, :] = hot(chosen == place)

    def edge_gather(target, first, start, count):
        place = lax.broadcasted_iota(jnp.int32, (lanes, count), 1)
        for row in range(edge_rows):
            chosen = index_columns[:, first + row : first + row + 1]
            target[row * lanes : (row + 1) * lanes, start : start + count] = hot(chosen == place)

    def edge_scatter(target, index, start, count):
        place = lax.broadcasted_iota(jnp.int32, (count, lanes), 0)
        for row in range(edge_rows):
            chosen = index[row : row + 1, :]
            target[start : start + count, row * lanes : (row + 1) * lanes] = hot(chosen == place)

    picks(grid_pick, 4 * edge_rows, slot_peer, grid_rows)

    arrive(grid_copies)
    proj_grid = matmul(grid_full[...], w_grid[...]).astype(jnp.bfloat16)
    outgoing[...] = matmul(grid_pick[...], proj_grid).astype(jnp.bfloat16)
    slot_copies = exchange(
        "band",
        lambda peer: outgoing.at[block(peer, slot_peer)],
        lambda me: enc_rows.at[block(me, slot_peer)],
    )
    enc_rows[block(band, slot_peer), :] = outgoing[block(band, slot_peer), :]
    arrive(mesh_copies)
    enc_full[block(feat, width), :] = w_enc_out[...]
    enc_weight_copies = exchange(
        "feat", lambda peer: w_enc_out, lambda me: enc_full.at[block(me, width)]
    )
    cot_copies = gather_columns(cotangent, cot_full)
    enc_rows[slots : slots + rows, :] = matmul(mesh_full[...], w_mesh[...]).astype(jnp.bfloat16)
    edge_gather(enc_gather, 0, 0, slots)
    edge_gather(enc_gather, edge_rows, slots, rows)
    edge_scatter(enc_scatter, g2m_dst, slots, rows)

    def per_chunk(body):
        size = 2 * lanes

        def step(place, carry):
            body(pl.ds(pl.multiple_of(place * size, size), size))
            return carry

        lax.fori_loop(0, edge_rows // 2, step, 0)

    arrive(slot_copies)

    def enc_forward(edges):
        values = matmul(enc_gather[edges, :], enc_rows[...])
        enc_pre[edges, :] = values
        edge_values[edges, :] = (values * sigmoid(values)).astype(jnp.bfloat16)

    per_chunk(enc_forward)
    enc_summed = matmul(enc_scatter[slots : slots + rows, :], edge_values[...])
    enc_whole[:, column(feat)] = enc_summed.astype(jnp.bfloat16)
    enc_copies = gather_held(enc_whole)

    def enc_slope(edges):
        enc_pre[edges, :] = silu_slope_of(enc_pre[edges, :])

    per_chunk(enc_slope)
    picks(mesh_pick, 4 * edge_rows + bands, halo_peer, rows)
    edge_gather(proc_gather, 2 * edge_rows, 0, ext)
    edge_gather(proc_gather, 3 * edge_rows, ext, rows)
    arrive(enc_weight_copies)
    arrive(enc_copies)
    mid_full[...] = (
        mesh_full[...].astype(jnp.float32) + matmul(enc_whole[...], enc_full[...])
    ).astype(jnp.bfloat16)
    proj_send = matmul(mid_full[...], w_send[...]).astype(jnp.bfloat16)
    halo_out[...] = matmul(mesh_pick[...], proj_send).astype(jnp.bfloat16)
    halo_copies = exchange(
        "band",
        lambda peer: halo_out.at[block(peer, halo_peer)],
        lambda me: proc_rows.at[pl.ds(pl.multiple_of(rows + me * halo_peer, halo_peer), halo_peer)],
    )
    send_weight_copies = gather_columns(w_send, send_full)
    recv_weight_copies = gather_columns(w_recv, recv_full)
    proc_rows[pl.ds(pl.multiple_of(rows + band * halo_peer, halo_peer), halo_peer), :] = halo_out[
        block(band, halo_peer), :
    ]
    proc_rows[0:rows, :] = proj_send
    proc_rows[ext : ext + rows, :] = matmul(mid_full[...], w_recv[...]).astype(jnp.bfloat16)
    arrive(cot_copies)
    back_proc = inner_columns(cot_full[...], w_proc_out[...]).astype(jnp.bfloat16)
    back_edge[...] = matmul(proc_gather[:, ext : ext + rows], back_proc)
    edge_scatter(proc_scatter, m2m_src, 0, ext)
    edge_scatter(proc_scatter, m2m_dst, ext, rows)
    arrive(halo_copies)

    def proc_forward(edges):
        values = matmul(proc_gather[edges, :], proc_rows[...])
        sigma = sigmoid(values)
        edge_values[edges, :] = (values * sigma).astype(jnp.bfloat16)
        slope = sigma * (1.0 + values * (1.0 - sigma))
        edge_slopes[edges, :] = (back_edge[edges, :] * slope).astype(jnp.bfloat16)

    per_chunk(proc_forward)
    back_ext[...] = matmul(proc_scatter[...], edge_slopes[...]).astype(jnp.bfloat16)
    halo_back_copies = exchange(
        "band",
        lambda peer: back_ext.at[pl.ds(pl.multiple_of(rows + peer * halo_peer, halo_peer), halo_peer)],
        lambda me: halo_back.at[block(me, halo_peer)],
    )
    halo_back[block(band, halo_peer), :] = back_ext[
        pl.ds(pl.multiple_of(rows + band * halo_peer, halo_peer), halo_peer), :
    ]
    recv_whole[:, column(feat)] = back_ext[ext : ext + rows, :]
    recv_copies = gather_held(recv_whole)
    proc_summed = matmul(proc_scatter[ext : ext + rows, :], edge_values[...]).astype(jnp.bfloat16)
    proc_whole[:, column(feat)] = proc_summed

    tall = tall_part.shape[1] // bands
    wide = wide_part.shape[1] // bands

    def scatter_sum(part, land, place, size, value):
        part[place] = value.astype(jnp.bfloat16)
        return exchange(
            "band",
            lambda peer: part.at[place, block(peer, size)],
            lambda me: land.at[place, me],
        )

    def add_up(copies, part, land, total, place, size):
        arrive(copies)
        mine = part[place, block(band, size), :]
        land[place, band] = mine
        value = land[place, 0].astype(jnp.float32)
        for other in range(1, bands):
            value = value + land[place, other].astype(jnp.float32)
        total[place, block(band, size), :] = (value * scale).astype(jnp.bfloat16)
        held = total.at[place, block(band, size)]
        return exchange("band", lambda peer: held, lambda me: held)

    grad_proc = scatter_sum(
        wide_part, wide_land, 0, wide, inner_rows(proc_summed, cot_full[...])
    )
    edge_scatter(enc_scatter, g2m_src, 0, slots)
    arrive(halo_back_copies)
    back_send = (
        back_ext[0:rows, :].astype(jnp.float32) + inner_rows(mesh_pick[...], halo_back[...])
    ).astype(jnp.bfloat16)
    send_whole[:, column(feat)] = back_send
    send_copies = gather_held(send_whole)
    proc_copies = gather_held(proc_whole)
    copies = exchange(
        "feat",
        lambda peer: w_proc_out.at[:, column(peer)],
        lambda me: proc_columns.at[block(me, width)],
    )
    proc_columns[block(feat, width), :] = w_proc_out[:, column(feat)]
    proc_copies = proc_copies + copies
    slice_copies = exchange(
        "feat",
        lambda peer: w_grid.at[block(peer, width)],
        lambda me: grid_slice.at[:, column(me)],
    )
    grid_slice[:, column(feat)] = w_grid[block(feat, width), :]
    grad_send = scatter_sum(tall_part, tall_land, 0, tall, inner_rows(mid_full[...], back_send))
    grad_recv = scatter_sum(
        tall_part, tall_land, 1, tall, inner_rows(mid_full[...], back_ext[ext : ext + rows, :])
    )
    arrive(send_weight_copies)
    arrive(recv_weight_copies)
    arrive(recv_copies)
    back_sum = cot_full[...].astype(jnp.float32) + inner_columns(recv_whole[...], recv_full[...])
    arrive(send_copies)
    back_full[...] = (back_sum + inner_columns(send_whole[...], send_full[...])).astype(
        jnp.bfloat16
    )
    back_enc = inner_columns(back_full[...], w_enc_out[...]).astype(jnp.bfloat16)
    back_edge[...] = matmul(enc_gather[:, slots : slots + rows], back_enc)

    def enc_backward(edges):
        edge_slopes[edges, :] = (back_edge[edges, :] * enc_pre[edges, :]).astype(jnp.bfloat16)

    per_chunk(enc_backward)
    back_slot[...] = matmul(enc_scatter[...], edge_slopes[...]).astype(jnp.bfloat16)
    slot_back_copies = exchange(
        "band",
        lambda peer: back_slot.at[block(peer, slot_peer)],
        lambda me: slot_back.at[block(me, slot_peer)],
    )
    slot_back[block(band, slot_peer), :] = back_slot[block(band, slot_peer), :]
    grad_mesh = scatter_sum(
        tall_part,
        tall_land,
        2,
        tall,
        inner_rows(mesh_full[...], back_slot[slots : slots + rows, :]),
    )
    grad_enc = scatter_sum(
        wide_part, wide_land, 1, wide, inner_rows(enc_whole[:, column(feat)], back_full[...])
    )
    proc_total = add_up(grad_proc, wide_part, wide_land, wide_sum, 0, wide)
    arrive(slot_back_copies)
    back_pgrid = inner_rows(grid_pick[...], slot_back[...]).astype(jnp.bfloat16)
    pgrid_whole[:, column(feat)] = back_pgrid
    grad_grid = scatter_sum(
        tall_part, tall_land, 3, tall, inner_rows(grid_full[...], back_pgrid)
    )
    pgrid_copies = gather_held(pgrid_whole)
    send_total = add_up(grad_send, tall_part, tall_land, tall_sum, 0, tall)
    recv_total = add_up(grad_recv, tall_part, tall_land, tall_sum, 1, tall)
    mesh_total = add_up(grad_mesh, tall_part, tall_land, tall_sum, 2, tall)
    enc_total = add_up(grad_enc, wide_part, wide_land, wide_sum, 1, wide)
    grid_total = add_up(grad_grid, tall_part, tall_land, tall_sum, 3, tall)
    arrive(proc_copies)
    mesh_out[...] = (
        mid_full[:, column(feat)].astype(jnp.float32)
        + matmul(proc_whole[...], proc_columns[...])
    ).astype(jnp.bfloat16)
    arrive(slice_copies)
    arrive(pgrid_copies)
    grid_grad[...] = inner_columns(pgrid_whole[...], grid_slice[...]).astype(jnp.bfloat16)
    for total, held, place, target in (
        (proc_total, wide_sum, 0, out_proc),
        (send_total, tall_sum, 0, out_send),
        (recv_total, tall_sum, 1, out_recv),
        (mesh_total, tall_sum, 2, out_mesh),
        (enc_total, wide_sum, 1, out_enc),
        (grid_total, tall_sum, 3, out_grid),
    ):
        arrive(total)
        target[...] = held[place].astype(target.dtype)
    for copy in started:
        copy.wait_send()


def silu_slope_of(values):
    sigma = sigmoid(values)
    return sigma * (1.0 + values * (1.0 - sigma))


def per_device(*arrays):
    (grid_latent, mesh_latent, w_grid, _, w_enc_out) = arrays[:5]
    grid_send, g2m_src, mesh_send = arrays[8], arrays[9], arrays[11]
    bands = lax.axis_size("band")
    feats = lax.axis_size("feat")
    slot_peer, halo_peer = grid_send.shape[1], mesh_send.shape[1]
    rows, width = mesh_latent.shape
    grid_rows = grid_latent.shape[0]
    latent = w_grid.shape[0]
    edge_rows, lanes = g2m_src.shape
    if slot_peer % 16 or halo_peer % 16 or width % (16 * bands) or 4 * edge_rows + 2 * bands > lanes:
        return per_device_collectives(*arrays)
    slots, halos = bands * slot_peer, bands * halo_peer
    ext = rows + halos
    edges = edge_rows * lanes
    scale = 1.0 / math.sqrt(rows * bands)

    def half(*shape):
        return pltpu.VMEM(shape, jnp.bfloat16)

    def full(*shape):
        return pltpu.VMEM(shape, jnp.float32)

    feat_phases, band_phases = 13, 16
    scratch = [
        pltpu.VMEM((lanes, lanes), jnp.int32),
        pltpu.VMEM((lanes, lanes), jnp.int32),
        half(grid_rows, latent),
        half(rows, latent),
        half(rows, latent),
        half(latent, latent),
        half(latent, latent),
        half(latent, latent),
        half(latent, width),
        half(width, latent),
        half(slots, grid_rows),
        half(halos, rows),
        half(edges, slots + rows),
        half(slots + rows, edges),
        half(edges, ext + rows),
        half(ext + rows, edges),
        half(slots + rows, width),
        half(ext + rows, width),
        half(slots, width),
        half(halos, width),
        full(edges, width),
        full(edges, width),
        half(edges, width),
        half(edges, width),
        half(rows, latent),
        half(rows, latent),
        half(rows, latent),
        half(rows, latent),
        half(rows, latent),
        half(rows, latent),
        half(ext + rows, width),
        half(halos, width),
        half(slots + rows, width),
        half(slots, width),
        half(grid_rows, latent),
        half(4, latent, width),
        half(4, bands, latent // bands, width),
        half(4, latent, width),
        half(2, width, latent),
        half(2, bands, width // bands, latent),
        half(2, width, latent),
        pltpu.SemaphoreType.DMA((feat_phases, feats - 1)),
        pltpu.SemaphoreType.DMA((feat_phases, feats - 1)),
        pltpu.SemaphoreType.DMA((band_phases, bands - 1)),
        pltpu.SemaphoreType.DMA((band_phases, bands - 1)),
    ]
    tall = jax.ShapeDtypeStruct((latent, width), jnp.float32)
    wide = jax.ShapeDtypeStruct((width, latent), jnp.float32)
    out_shape = (
        jax.ShapeDtypeStruct((rows, width), jnp.bfloat16),
        jax.ShapeDtypeStruct((grid_rows, width), jnp.bfloat16),
        tall,
        tall,
        wide,
        tall,
        tall,
        wide,
    )
    vmem = pl.BlockSpec(memory_space=pltpu.VMEM)
    return pl.pallas_call(
        functools.partial(fused_kernel, bands, feats, scale),
        out_shape=out_shape,
        in_specs=[vmem] * len(arrays),
        out_specs=(vmem,) * len(out_shape),
        scratch_shapes=scratch,
        compiler_params=pltpu.CompilerParams(
            collective_id=0, has_side_effects=True, vmem_limit_bytes=48 * 1024 * 1024
        ),
    )(*arrays)


def solution(mesh):
    in_specs = (
        P("band", "feat"),
        P("band", "feat"),
        P(None, "feat"),
        P(None, "feat"),
        P("feat", None),
        P(None, "feat"),
        P(None, "feat"),
        P("feat", None),
        P("band", None),
        P("band", None),
        P("band", None),
        P("band", None),
        P("band", None),
        P("band", None),
        P("band", "feat"),
    )
    out_specs = (
        P("band", "feat"),
        P("band", "feat"),
        P(None, "feat"),
        P(None, "feat"),
        P("feat", None),
        P(None, "feat"),
        P(None, "feat"),
        P("feat", None),
    )
    return jax.shard_map(
        per_device, mesh=mesh, in_specs=in_specs, out_specs=out_specs, check_vma=False
    )
```

```python
import functools
import math

import jax
import jax.numpy as jnp
from jax import lax
from jax.experimental import pallas as pl
from jax.experimental.pallas import tpu as pltpu
from jax.sharding import PartitionSpec as P


def silu_slope(values):
    sigma = jax.nn.sigmoid(values)
    return sigma * (1.0 + values * (1.0 - sigma))


def matmul(left, right):
    return jnp.dot(left, right, preferred_element_type=jnp.float32)


def inner_rows(left, right):
    return lax.dot_general(
        left, right, (((0,), (0,)), ((), ())), preferred_element_type=jnp.float32
    )


def hot_table(index, count):
    return (index[:, None] == lax.iota(jnp.int32, count)[None, :]).astype(jnp.bfloat16)


def per_device_collectives(
    grid_latent,
    mesh_latent,
    w_grid,
    w_mesh,
    w_enc_out,
    w_send,
    w_recv,
    w_proc_out,
    grid_send,
    g2m_src,
    g2m_dst,
    mesh_send,
    m2m_src,
    m2m_dst,
    cotangent,
):
    bands = lax.axis_size("band")
    grid_rows = grid_latent.shape[0]
    mesh_rows = mesh_latent.shape[0]
    hidden_dev = w_grid.shape[1]
    halo_rows = bands * mesh_send.shape[1]
    slot_rows = bands * grid_send.shape[1]
    scale = 1.0 / math.sqrt(mesh_rows * bands)
    enc_source = g2m_src.reshape(-1)
    enc_target = g2m_dst.reshape(-1)
    proc_source = m2m_src.reshape(-1)
    proc_target = m2m_dst.reshape(-1)
    enc_columns, proc_columns = (
        lax.all_to_all(w_enc_out, "feat", split_axis=1, concat_axis=0, tiled=True),
        lax.all_to_all(w_proc_out, "feat", split_axis=1, concat_axis=0, tiled=True),
    )
    send_slice, recv_slice, grid_slice = (
        lax.all_to_all(w_send, "feat", split_axis=0, concat_axis=1, tiled=True),
        lax.all_to_all(w_recv, "feat", split_axis=0, concat_axis=1, tiled=True),
        lax.all_to_all(w_grid, "feat", split_axis=0, concat_axis=1, tiled=True),
    )
    grid_full = lax.all_gather(grid_latent, "feat", axis=1, tiled=True)
    mesh_full = lax.all_gather(mesh_latent, "feat", axis=1, tiled=True)
    proj_grid = matmul(grid_full, w_grid).astype(jnp.bfloat16)
    outgoing = jnp.take(proj_grid, grid_send, axis=0)
    arrived = lax.all_to_all(outgoing, "band", split_axis=0, concat_axis=0, tiled=True)
    slot_proj = arrived.reshape(slot_rows, hidden_dev)
    proj_mesh = matmul(mesh_full, w_mesh).astype(jnp.bfloat16)
    enc_pre = jnp.take(slot_proj, enc_source, axis=0).astype(jnp.float32) + jnp.take(
        proj_mesh, enc_target, axis=0
    ).astype(jnp.float32)
    enc_active = jax.nn.silu(enc_pre).astype(jnp.bfloat16)
    enc_table = hot_table(enc_target, mesh_rows)
    enc_summed = inner_rows(enc_table, enc_active).astype(jnp.bfloat16)
    enc_whole = lax.all_gather(enc_summed, "feat", axis=1, tiled=True)
    update = matmul(enc_whole, enc_columns)
    mesh_mid = (mesh_latent.astype(jnp.float32) + update).astype(jnp.bfloat16)
    mid_full = lax.all_gather(mesh_mid, "feat", axis=1, tiled=True)
    proj_send = matmul(mid_full, w_send).astype(jnp.bfloat16)
    proj_recv = matmul(mid_full, w_recv).astype(jnp.bfloat16)
    halo_out = jnp.take(proj_send, mesh_send, axis=0)
    halo_in = lax.all_to_all(halo_out, "band", split_axis=0, concat_axis=0, tiled=True)
    extended = jnp.concatenate([proj_send, halo_in.reshape(halo_rows, hidden_dev)], axis=0)
    proc_pre = jnp.take(extended, proc_source, axis=0).astype(jnp.float32) + jnp.take(
        proj_recv, proc_target, axis=0
    ).astype(jnp.float32)
    proc_active = jax.nn.silu(proc_pre).astype(jnp.bfloat16)
    proc_table = hot_table(proc_target, mesh_rows)
    proc_summed = inner_rows(proc_table, proc_active).astype(jnp.bfloat16)
    proc_whole = lax.all_gather(proc_summed, "feat", axis=1, tiled=True)
    proc_update = matmul(proc_whole, proc_columns)
    mesh_out = (mesh_mid.astype(jnp.float32) + proc_update).astype(jnp.bfloat16)
    cot_full = lax.all_gather(cotangent, "feat", axis=1, tiled=True)
    back_proc = matmul(cot_full, w_proc_out.T).astype(jnp.bfloat16)
    grad_proc_out = inner_rows(proc_summed, cot_full)
    slope_proc = (
        jnp.take(back_proc, proc_target, axis=0).astype(jnp.float32) * silu_slope(proc_pre)
    ).astype(jnp.bfloat16)
    back_recv = inner_rows(proc_table, slope_proc).astype(jnp.bfloat16)
    source_table = hot_table(proc_source, mesh_rows + halo_rows)
    back_ext = inner_rows(source_table, slope_proc).astype(jnp.bfloat16)
    back_halo = back_ext[mesh_rows:].reshape(bands, halo_rows // bands, hidden_dev)
    returned = lax.all_to_all(back_halo, "band", split_axis=0, concat_axis=0, tiled=True)
    returned_sum = jax.ops.segment_sum(
        returned.reshape(halo_rows, hidden_dev).astype(jnp.float32),
        mesh_send.reshape(-1),
        num_segments=mesh_rows,
    )
    back_send = (back_ext[:mesh_rows].astype(jnp.float32) + returned_sum).astype(jnp.bfloat16)
    grad_send = inner_rows(mid_full, back_send)
    grad_recv = inner_rows(mid_full, back_recv)
    send_whole, recv_whole = (
        lax.all_gather(back_send, "feat", axis=1, tiled=True),
        lax.all_gather(back_recv, "feat", axis=1, tiled=True),
    )
    back_sum = matmul(send_whole, send_slice.T) + matmul(recv_whole, recv_slice.T)
    back_mid = (cotangent.astype(jnp.float32) + back_sum).astype(jnp.bfloat16)
    back_full = lax.all_gather(back_mid, "feat", axis=1, tiled=True)
    back_enc = matmul(back_full, w_enc_out.T).astype(jnp.bfloat16)
    grad_enc_out = inner_rows(enc_summed, back_full)
    slope_enc = (
        jnp.take(back_enc, enc_target, axis=0).astype(jnp.float32) * silu_slope(enc_pre)
    ).astype(jnp.bfloat16)
    back_pmesh = inner_rows(enc_table, slope_enc).astype(jnp.bfloat16)
    grad_mesh_w = inner_rows(mesh_full, back_pmesh)
    slot_table = hot_table(enc_source, slot_rows)
    back_slot = inner_rows(slot_table, slope_enc).astype(jnp.bfloat16)
    back_slots = lax.all_to_all(
        back_slot.reshape(bands, slot_rows // bands, hidden_dev),
        "band",
        split_axis=0,
        concat_axis=0,
        tiled=True,
    )
    back_pgrid = jax.ops.segment_sum(
        back_slots.reshape(slot_rows, hidden_dev).astype(jnp.float32),
        grid_send.reshape(-1),
        num_segments=grid_rows,
    ).astype(jnp.bfloat16)
    grad_grid_w = inner_rows(grid_full, back_pgrid)
    pgrid_whole = lax.all_gather(back_pgrid, "feat", axis=1, tiled=True)
    grid_grad = matmul(pgrid_whole, grid_slice.T).astype(jnp.bfloat16)
    grad_grid_w, grad_mesh_w, grad_enc_out, grad_send, grad_recv, grad_proc_out = lax.psum(
        (grad_grid_w, grad_mesh_w, grad_enc_out, grad_send, grad_recv, grad_proc_out), "band"
    )
    return (
        mesh_out,
        grid_grad,
        grad_grid_w * scale,
        grad_mesh_w * scale,
        grad_enc_out * scale,
        grad_send * scale,
        grad_recv * scale,
        grad_proc_out * scale,
    )


def inner_columns(left, right):
    return lax.dot_general(
        left, right, (((1,), (1,)), ((), ())), preferred_element_type=jnp.float32
    )


def hot(condition):
    return jnp.where(condition, 1.0, 0.0).astype(jnp.bfloat16)


def sigmoid(values):
    return 1.0 / (1.0 + jnp.exp(-values))


def fused_kernel(
    bands,
    feats,
    scale,
    grid_latent,
    mesh_latent,
    w_grid_hbm,
    w_mesh_hbm,
    w_enc_hbm,
    w_send_hbm,
    w_recv_hbm,
    w_proc_hbm,
    grid_send_hbm,
    g2m_src,
    g2m_dst,
    mesh_send_hbm,
    m2m_src,
    m2m_dst,
    cotangent,
    mesh_out,
    grid_grad,
    tall_out,
    wide_out,
    w_grid,
    w_mesh,
    w_proc_out,
    grid_send,
    mesh_send,
    index_rows,
    index_columns,
    grid_full,
    mesh_full,
    cot_full,
    enc_full,
    send_full,
    recv_full,
    proc_columns,
    grid_slice,
    grid_pick,
    mesh_pick,
    enc_gather,
    enc_scatter,
    proc_gather,
    proc_scatter,
    enc_rows,
    proc_rows,
    outgoing,
    halo_out,
    enc_pre,
    back_edge,
    edge_values,
    edge_slopes,
    enc_whole,
    mid_full,
    proc_whole,
    recv_whole,
    send_whole,
    back_full,
    back_ext,
    halo_back,
    back_slot,
    slot_back,
    pgrid_whole,
    tall_part,
    tall_land,
    tall_sum,
    wide_part,
    wide_land,
    wide_sum,
    feat_send_sem,
    feat_recv_sem,
    band_send_sem,
    band_recv_sem,
    stage_sem,
):
    band = lax.axis_index("band")
    feat = lax.axis_index("feat")
    width = grid_latent.shape[1]
    rows = mesh_latent.shape[0]
    grid_rows = grid_latent.shape[0]
    slot_peer = grid_send.shape[1]
    halo_peer = mesh_send.shape[1]
    slots = bands * slot_peer
    halos = bands * halo_peer
    edge_rows = g2m_src.shape[0]
    lanes = g2m_src.shape[1]
    ext = rows + halos
    started = []

    def column(place):
        return pl.ds(pl.multiple_of(place * width, width), width)

    def block(place, size):
        return pl.ds(pl.multiple_of(place * size, size), size)

    staged = []

    def stage(source, target):
        copy = pltpu.make_async_copy(source, target, stage_sem.at[len(staged)])
        copy.start()
        staged.append(copy)
        return copy

    index_rows[...] = jnp.zeros_like(index_rows)
    index_copies = [
        stage(source, index_rows.at[pl.ds(place * edge_rows, edge_rows)])
        for place, source in enumerate((g2m_src, g2m_dst, m2m_src, m2m_dst))
    ]
    index_copies += [stage(grid_send_hbm, grid_send), stage(mesh_send_hbm, mesh_send)]
    w_grid_copy = stage(w_grid_hbm, w_grid)
    grid_own = stage(grid_latent, grid_full.at[:, column(feat)])
    mesh_own = stage(mesh_latent, mesh_full.at[:, column(feat)])
    w_mesh_copy = stage(w_mesh_hbm, w_mesh)
    enc_own = stage(w_enc_hbm, enc_full.at[block(feat, width)])
    cot_own = stage(cotangent, cot_full.at[:, column(feat)])
    w_proc_copy = stage(w_proc_hbm, w_proc_out)
    send_own = stage(w_send_hbm, send_full.at[:, column(feat)])
    recv_own = stage(w_recv_hbm, recv_full.at[:, column(feat)])

    barrier = pltpu.get_barrier_semaphore()
    for step in range(1, bands):
        pl.semaphore_signal(
            barrier,
            inc=1,
            device_id={"band": lax.rem(band + step, bands)},
            device_id_type=pl.DeviceIdType.MESH,
        )
    for step in range(1, feats):
        pl.semaphore_signal(
            barrier,
            inc=1,
            device_id={"feat": lax.rem(feat + step, feats)},
            device_id_type=pl.DeviceIdType.MESH,
        )
    pl.semaphore_wait(barrier, bands + feats - 2)

    counts = {"feat": 0, "band": 0}

    def exchange(axis, source, target):
        me, size, send_sem, recv_sem = (
            (feat, feats, feat_send_sem, feat_recv_sem)
            if axis == "feat"
            else (band, bands, band_send_sem, band_recv_sem)
        )
        phase = counts[axis]
        counts[axis] += 1
        copies = []
        for step in range(1, size):
            peer = lax.rem(me + step, size)
            copy = pltpu.make_async_remote_copy(
                src_ref=source(peer),
                dst_ref=target(me),
                send_sem=send_sem.at[phase, step - 1],
                recv_sem=recv_sem.at[phase, step - 1],
                device_id={axis: peer},
                device_id_type=pl.DeviceIdType.MESH,
            )
            copy.start()
            copies.append(copy)
        started.extend(copies)
        return copies

    def arrive(copies):
        for copy in copies:
            copy.wait_recv()

    def gather_columns(source, target):
        return exchange("feat", lambda peer: source, lambda me: target.at[:, column(me)])

    def gather_held(target):
        mine = target.at[:, column(feat)]
        return exchange("feat", lambda peer: mine, lambda me: mine)

    grid_copies = gather_columns(grid_latent, grid_full)
    mesh_copies = gather_columns(mesh_latent, mesh_full)

    for copy in index_copies:
        copy.wait()
    index_rows[4 * edge_rows : 4 * edge_rows + bands, 0:slot_peer] = grid_send[...]
    index_rows[4 * edge_rows + bands : 4 * edge_rows + 2 * bands, 0:halo_peer] = mesh_send[...]
    index_columns[...] = index_rows[...].T

    def picks(target, first, size, count):
        place = lax.broadcasted_iota(jnp.int32, (size, count), 1)
        for peer in range(bands):
            chosen = index_columns[0:size, first + peer : first + peer + 1]
            target[peer * size : (peer + 1) * size, :] = hot(chosen == place)

    def edge_gather(target, first, start, count):
        place = lax.broadcasted_iota(jnp.int32, (lanes, count), 1)
        for row in range(edge_rows):
            chosen = index_columns[:, first + row : first + row + 1]
            target[row * lanes : (row + 1) * lanes, start : start + count] = hot(chosen == place)

    def edge_scatter(target, index, start, count):
        place = lax.broadcasted_iota(jnp.int32, (count, lanes), 0)
        for row in range(edge_rows):
            chosen = index_rows[index + row : index + row + 1, :]
            target[start : start + count, row * lanes : (row + 1) * lanes] = hot(chosen == place)

    picks(grid_pick, 4 * edge_rows, slot_peer, grid_rows)

    grid_own.wait()
    w_grid_copy.wait()
    arrive(grid_copies)
    proj_grid = matmul(grid_full[...], w_grid[...]).astype(jnp.bfloat16)
    outgoing[...] = matmul(grid_pick[...], proj_grid).astype(jnp.bfloat16)
    slot_copies = exchange(
        "band",
        lambda peer: outgoing.at[block(peer, slot_peer)],
        lambda me: enc_rows.at[block(me, slot_peer)],
    )
    enc_rows[block(band, slot_peer), :] = outgoing[block(band, slot_peer), :]
    mesh_own.wait()
    w_mesh_copy.wait()
    arrive(mesh_copies)
    enc_weight_copies = exchange(
        "feat", lambda peer: w_enc_hbm, lambda me: enc_full.at[block(me, width)]
    )
    cot_copies = gather_columns(cotangent, cot_full)
    enc_rows[slots : slots + rows, :] = matmul(mesh_full[...], w_mesh[...]).astype(jnp.bfloat16)
    edge_gather(enc_gather, 0, 0, slots)
    edge_gather(enc_gather, edge_rows, slots, rows)
    edge_scatter(enc_scatter, edge_rows, slots, rows)

    def per_chunk(body):
        size = 2 * lanes

        def step(place, carry):
            body(pl.ds(pl.multiple_of(place * size, size), size))
            return carry

        lax.fori_loop(0, edge_rows // 2, step, 0)

    arrive(slot_copies)

    def enc_forward(edges):
        values = matmul(enc_gather[edges, :], enc_rows[...])
        enc_pre[edges, :] = values
        edge_values[edges, :] = (values * sigmoid(values)).astype(jnp.bfloat16)

    per_chunk(enc_forward)
    enc_summed = matmul(enc_scatter[slots : slots + rows, :], edge_values[...])
    enc_whole[:, column(feat)] = enc_summed.astype(jnp.bfloat16)
    enc_copies = gather_held(enc_whole)

    def enc_slope(edges):
        enc_pre[edges, :] = silu_slope_of(enc_pre[edges, :])

    per_chunk(enc_slope)
    picks(mesh_pick, 4 * edge_rows + bands, halo_peer, rows)
    edge_gather(proc_gather, 2 * edge_rows, 0, ext)
    edge_gather(proc_gather, 3 * edge_rows, ext, rows)
    enc_own.wait()
    arrive(enc_weight_copies)
    arrive(enc_copies)
    send_own.wait()
    mid_full[...] = (
        mesh_full[...].astype(jnp.float32) + matmul(enc_whole[...], enc_full[...])
    ).astype(jnp.bfloat16)
    proj_send = matmul(mid_full[...], send_full[:, column(feat)]).astype(jnp.bfloat16)
    halo_out[...] = matmul(mesh_pick[...], proj_send).astype(jnp.bfloat16)
    halo_copies = exchange(
        "band",
        lambda peer: halo_out.at[block(peer, halo_peer)],
        lambda me: proc_rows.at[pl.ds(pl.multiple_of(rows + me * halo_peer, halo_peer), halo_peer)],
    )
    send_weight_copies = gather_columns(w_send_hbm, send_full)
    recv_weight_copies = gather_columns(w_recv_hbm, recv_full)
    recv_own.wait()
    proc_rows[pl.ds(pl.multiple_of(rows + band * halo_peer, halo_peer), halo_peer), :] = halo_out[
        block(band, halo_peer), :
    ]
    proc_rows[0:rows, :] = proj_send
    proc_rows[ext : ext + rows, :] = matmul(mid_full[...], recv_full[:, column(feat)]).astype(jnp.bfloat16)
    cot_own.wait()
    w_proc_copy.wait()
    arrive(cot_copies)
    back_proc = inner_columns(cot_full[...], w_proc_out[...]).astype(jnp.bfloat16)
    back_edge[...] = matmul(proc_gather[:, ext : ext + rows], back_proc)
    edge_scatter(proc_scatter, 2 * edge_rows, 0, ext)
    edge_scatter(proc_scatter, 3 * edge_rows, ext, rows)
    arrive(halo_copies)

    def proc_forward(edges):
        values = matmul(proc_gather[edges, :], proc_rows[...])
        sigma = sigmoid(values)
        edge_values[edges, :] = (values * sigma).astype(jnp.bfloat16)
        slope = sigma * (1.0 + values * (1.0 - sigma))
        edge_slopes[edges, :] = (back_edge[edges, :] * slope).astype(jnp.bfloat16)

    per_chunk(proc_forward)
    back_ext[...] = matmul(proc_scatter[...], edge_slopes[...]).astype(jnp.bfloat16)
    halo_back_copies = exchange(
        "band",
        lambda peer: back_ext.at[pl.ds(pl.multiple_of(rows + peer * halo_peer, halo_peer), halo_peer)],
        lambda me: halo_back.at[block(me, halo_peer)],
    )
    halo_back[block(band, halo_peer), :] = back_ext[
        pl.ds(pl.multiple_of(rows + band * halo_peer, halo_peer), halo_peer), :
    ]
    recv_whole[:, column(feat)] = back_ext[ext : ext + rows, :]
    recv_copies = gather_held(recv_whole)
    proc_summed = matmul(proc_scatter[ext : ext + rows, :], edge_values[...]).astype(jnp.bfloat16)
    proc_whole[:, column(feat)] = proc_summed

    tall = tall_part.shape[1] // bands
    wide = wide_part.shape[1] // bands

    def scatter_sum(part, land, place, size, value):
        part[place] = value.astype(jnp.bfloat16)
        return exchange(
            "band",
            lambda peer: part.at[place, block(peer, size)],
            lambda me: land.at[place, me],
        )

    def add_up(copies, part, land, total, place, size):
        arrive(copies)
        mine = part[place, block(band, size), :]
        land[place, band] = mine
        value = land[place, 0].astype(jnp.float32)
        for other in range(1, bands):
            value = value + land[place, other].astype(jnp.float32)
        total[place, block(band, size), :] = (value * scale).astype(jnp.bfloat16)
        held = total.at[place, block(band, size)]
        return exchange("band", lambda peer: held, lambda me: held)

    grad_proc = scatter_sum(
        wide_part, wide_land, 0, wide, inner_rows(proc_summed, cot_full[...])
    )
    edge_scatter(enc_scatter, 0, 0, slots)
    arrive(halo_back_copies)
    back_send = (
        back_ext[0:rows, :].astype(jnp.float32) + inner_rows(mesh_pick[...], halo_back[...])
    ).astype(jnp.bfloat16)
    send_whole[:, column(feat)] = back_send
    send_copies = gather_held(send_whole)
    proc_copies = gather_held(proc_whole)
    copies = exchange(
        "feat",
        lambda peer: w_proc_out.at[:, column(peer)],
        lambda me: proc_columns.at[block(me, width)],
    )
    proc_columns[block(feat, width), :] = w_proc_out[:, column(feat)]
    proc_copies = proc_copies + copies
    slice_copies = exchange(
        "feat",
        lambda peer: w_grid.at[block(peer, width)],
        lambda me: grid_slice.at[:, column(me)],
    )
    grid_slice[:, column(feat)] = w_grid[block(feat, width), :]
    grad_send = scatter_sum(tall_part, tall_land, 0, tall, inner_rows(mid_full[...], back_send))
    grad_recv = scatter_sum(
        tall_part, tall_land, 1, tall, inner_rows(mid_full[...], back_ext[ext : ext + rows, :])
    )
    arrive(send_weight_copies)
    arrive(recv_weight_copies)
    arrive(recv_copies)
    back_sum = cot_full[...].astype(jnp.float32) + inner_columns(recv_whole[...], recv_full[...])
    arrive(send_copies)
    back_full[...] = (back_sum + inner_columns(send_whole[...], send_full[...])).astype(
        jnp.bfloat16
    )
    back_enc = inner_columns(back_full[...], enc_full[block(feat, width), :]).astype(jnp.bfloat16)
    back_edge[...] = matmul(enc_gather[:, slots : slots + rows], back_enc)

    def enc_backward(edges):
        edge_slopes[edges, :] = (back_edge[edges, :] * enc_pre[edges, :]).astype(jnp.bfloat16)

    per_chunk(enc_backward)
    back_slot[...] = matmul(enc_scatter[...], edge_slopes[...]).astype(jnp.bfloat16)
    slot_back_copies = exchange(
        "band",
        lambda peer: back_slot.at[block(peer, slot_peer)],
        lambda me: slot_back.at[block(me, slot_peer)],
    )
    slot_back[block(band, slot_peer), :] = back_slot[block(band, slot_peer), :]
    grad_mesh = scatter_sum(
        tall_part,
        tall_land,
        2,
        tall,
        inner_rows(mesh_full[...], back_slot[slots : slots + rows, :]),
    )
    grad_enc = scatter_sum(
        wide_part, wide_land, 1, wide, inner_rows(enc_whole[:, column(feat)], back_full[...])
    )
    proc_total = add_up(grad_proc, wide_part, wide_land, wide_sum, 0, wide)
    arrive(slot_back_copies)
    back_pgrid = inner_rows(grid_pick[...], slot_back[...]).astype(jnp.bfloat16)
    pgrid_whole[:, column(feat)] = back_pgrid
    grad_grid = scatter_sum(
        tall_part, tall_land, 3, tall, inner_rows(grid_full[...], back_pgrid)
    )
    pgrid_copies = gather_held(pgrid_whole)
    send_total = add_up(grad_send, tall_part, tall_land, tall_sum, 0, tall)
    recv_total = add_up(grad_recv, tall_part, tall_land, tall_sum, 1, tall)
    mesh_total = add_up(grad_mesh, tall_part, tall_land, tall_sum, 2, tall)
    enc_total = add_up(grad_enc, wide_part, wide_land, wide_sum, 1, wide)
    grid_total = add_up(grad_grid, tall_part, tall_land, tall_sum, 3, tall)
    arrive(proc_copies)
    mesh_out[...] = (
        mid_full[:, column(feat)].astype(jnp.float32)
        + matmul(proc_whole[...], proc_columns[...])
    ).astype(jnp.bfloat16)
    arrive(slice_copies)
    arrive(pgrid_copies)
    grid_grad[...] = inner_columns(pgrid_whole[...], grid_slice[...]).astype(jnp.bfloat16)
    for total in (proc_total, send_total, recv_total, mesh_total, enc_total, grid_total):
        arrive(total)
    tall_out[...] = tall_sum[...]
    wide_out[...] = wide_sum[...]
    for copy in started:
        copy.wait_send()


def write_kernel(
    mesh_held,
    grid_held,
    tall_hbm,
    wide_hbm,
    mesh_out,
    grid_grad,
    out_grid,
    out_mesh,
    out_enc,
    out_send,
    out_recv,
    out_proc,
    tall_held,
    wide_held,
    tall_wide,
    wide_wide,
    copy_sem,
    load_sem,
):
    loads = [
        pltpu.make_async_copy(tall_hbm, tall_held, load_sem.at[0]),
        pltpu.make_async_copy(wide_hbm, wide_held, load_sem.at[1]),
    ]
    for load in loads:
        load.start()
    copies = [
        pltpu.make_async_copy(mesh_held, mesh_out, copy_sem.at[0]),
        pltpu.make_async_copy(grid_held, grid_grad, copy_sem.at[1]),
    ]
    for copy in copies:
        copy.start()
    for load in loads:
        load.wait()
    for held, wide, place, target in (
        (tall_held, tall_wide, 0, out_send),
        (tall_held, tall_wide, 1, out_recv),
        (tall_held, tall_wide, 2, out_mesh),
        (tall_held, tall_wide, 3, out_grid),
        (wide_held, wide_wide, 0, out_proc),
        (wide_held, wide_wide, 1, out_enc),
    ):
        wide[place] = held[place].astype(jnp.float32)
        copy = pltpu.make_async_copy(wide.at[place], target, copy_sem.at[len(copies)])
        copy.start()
        copies.append(copy)
    for copy in copies:
        copy.wait()


def silu_slope_of(values):
    sigma = sigmoid(values)
    return sigma * (1.0 + values * (1.0 - sigma))


def per_device(*arrays):
    (grid_latent, mesh_latent, w_grid, _, w_enc_out) = arrays[:5]
    grid_send, g2m_src, mesh_send = arrays[8], arrays[9], arrays[11]
    bands = lax.axis_size("band")
    feats = lax.axis_size("feat")
    slot_peer, halo_peer = grid_send.shape[1], mesh_send.shape[1]
    rows, width = mesh_latent.shape
    grid_rows = grid_latent.shape[0]
    latent = w_grid.shape[0]
    edge_rows, lanes = g2m_src.shape
    if edge_rows % 8 or slot_peer % 16 or halo_peer % 16 or width % (16 * bands) or 4 * edge_rows + 2 * bands > lanes:
        return per_device_collectives(*arrays)
    slots, halos = bands * slot_peer, bands * halo_peer
    ext = rows + halos
    edges = edge_rows * lanes
    scale = 1.0 / math.sqrt(rows * bands)

    def half(*shape):
        return pltpu.VMEM(shape, jnp.bfloat16)

    def full(*shape):
        return pltpu.VMEM(shape, jnp.float32)

    feat_phases, band_phases = 13, 16
    scratch = [
        half(latent, width),
        half(latent, width),
        half(width, latent),
        pltpu.VMEM(grid_send.shape, jnp.int32),
        pltpu.VMEM(mesh_send.shape, jnp.int32),
        pltpu.VMEM((lanes, lanes), jnp.int32),
        pltpu.VMEM((lanes, lanes), jnp.int32),
        half(grid_rows, latent),
        half(rows, latent),
        half(rows, latent),
        half(latent, latent),
        half(latent, latent),
        half(latent, latent),
        half(latent, width),
        half(width, latent),
        half(slots, grid_rows),
        half(halos, rows),
        half(edges, slots + rows),
        half(slots + rows, edges),
        half(edges, ext + rows),
        half(ext + rows, edges),
        half(slots + rows, width),
        half(ext + rows, width),
        half(slots, width),
        half(halos, width),
        full(edges, width),
        full(edges, width),
        half(edges, width),
        half(edges, width),
        half(rows, latent),
        half(rows, latent),
        half(rows, latent),
        half(rows, latent),
        half(rows, latent),
        half(rows, latent),
        half(ext + rows, width),
        half(halos, width),
        half(slots + rows, width),
        half(slots, width),
        half(grid_rows, latent),
        half(4, latent, width),
        half(4, bands, latent // bands, width),
        half(4, latent, width),
        half(2, width, latent),
        half(2, bands, width // bands, latent),
        half(2, width, latent),
        pltpu.SemaphoreType.DMA((feat_phases, feats - 1)),
        pltpu.SemaphoreType.DMA((feat_phases, feats - 1)),
        pltpu.SemaphoreType.DMA((band_phases, bands - 1)),
        pltpu.SemaphoreType.DMA((band_phases, bands - 1)),
        pltpu.SemaphoreType.DMA((len(arrays),)),
    ]
    tall = jax.ShapeDtypeStruct((latent, width), jnp.float32)
    wide = jax.ShapeDtypeStruct((width, latent), jnp.float32)
    nodes = (
        jax.ShapeDtypeStruct((rows, width), jnp.bfloat16),
        jax.ShapeDtypeStruct((grid_rows, width), jnp.bfloat16),
    )
    sums = (
        jax.ShapeDtypeStruct((4, latent, width), jnp.bfloat16),
        jax.ShapeDtypeStruct((2, width, latent), jnp.bfloat16),
    )
    vmem = pl.BlockSpec(memory_space=pltpu.VMEM)
    hbm = pl.BlockSpec(memory_space=pltpu.HBM)
    held = pl.pallas_call(
        functools.partial(fused_kernel, bands, feats, scale),
        out_shape=nodes + sums,
        in_specs=[hbm] * len(arrays),
        out_specs=(vmem,) * 4,
        scratch_shapes=scratch,
        compiler_params=pltpu.CompilerParams(
            collective_id=0, has_side_effects=True, vmem_limit_bytes=61 * 1024 * 1024
        ),
    )(*arrays)
    return pl.pallas_call(
        write_kernel,
        out_shape=nodes + (tall, tall, wide, tall, tall, wide),
        in_specs=[hbm] * 4,
        out_specs=(hbm,) * 8,
        scratch_shapes=[
            half(4, latent, width),
            half(2, width, latent),
            full(4, latent, width),
            full(2, width, latent),
            pltpu.SemaphoreType.DMA((8,)),
            pltpu.SemaphoreType.DMA((2,)),
        ],
        compiler_params=pltpu.CompilerParams(vmem_limit_bytes=61 * 1024 * 1024),
    )(*held)


def solution(mesh):
    in_specs = (
        P("band", "feat"),
        P("band", "feat"),
        P(None, "feat"),
        P(None, "feat"),
        P("feat", None),
        P(None, "feat"),
        P(None, "feat"),
        P("feat", None),
        P("band", None),
        P("band", None),
        P("band", None),
        P("band", None),
        P("band", None),
        P("band", None),
        P("band", "feat"),
    )
    out_specs = (
        P("band", "feat"),
        P("band", "feat"),
        P(None, "feat"),
        P(None, "feat"),
        P("feat", None),
        P(None, "feat"),
        P(None, "feat"),
        P("feat", None),
    )
    return jax.shard_map(
        per_device, mesh=mesh, in_specs=in_specs, out_specs=out_specs, check_vma=False
    )
```

```python
import functools
import math

import jax
import jax.numpy as jnp
from jax import lax
from jax.experimental import pallas as pl
from jax.experimental.pallas import tpu as pltpu
from jax.sharding import PartitionSpec as P


def silu_slope(values):
    sigma = jax.nn.sigmoid(values)
    return sigma * (1.0 + values * (1.0 - sigma))


def matmul(left, right):
    return jnp.dot(left, right, preferred_element_type=jnp.float32)


def inner_rows(left, right):
    return lax.dot_general(
        left, right, (((0,), (0,)), ((), ())), preferred_element_type=jnp.float32
    )


def hot_table(index, count):
    return (index[:, None] == lax.iota(jnp.int32, count)[None, :]).astype(jnp.bfloat16)


def per_device_collectives(
    grid_latent,
    mesh_latent,
    w_grid,
    w_mesh,
    w_enc_out,
    w_send,
    w_recv,
    w_proc_out,
    grid_send,
    g2m_src,
    g2m_dst,
    mesh_send,
    m2m_src,
    m2m_dst,
    cotangent,
):
    bands = lax.axis_size("band")
    grid_rows = grid_latent.shape[0]
    mesh_rows = mesh_latent.shape[0]
    hidden_dev = w_grid.shape[1]
    halo_rows = bands * mesh_send.shape[1]
    slot_rows = bands * grid_send.shape[1]
    scale = 1.0 / math.sqrt(mesh_rows * bands)
    enc_source = g2m_src.reshape(-1)
    enc_target = g2m_dst.reshape(-1)
    proc_source = m2m_src.reshape(-1)
    proc_target = m2m_dst.reshape(-1)
    enc_columns, proc_columns = (
        lax.all_to_all(w_enc_out, "feat", split_axis=1, concat_axis=0, tiled=True),
        lax.all_to_all(w_proc_out, "feat", split_axis=1, concat_axis=0, tiled=True),
    )
    send_slice, recv_slice, grid_slice = (
        lax.all_to_all(w_send, "feat", split_axis=0, concat_axis=1, tiled=True),
        lax.all_to_all(w_recv, "feat", split_axis=0, concat_axis=1, tiled=True),
        lax.all_to_all(w_grid, "feat", split_axis=0, concat_axis=1, tiled=True),
    )
    grid_full = lax.all_gather(grid_latent, "feat", axis=1, tiled=True)
    mesh_full = lax.all_gather(mesh_latent, "feat", axis=1, tiled=True)
    proj_grid = matmul(grid_full, w_grid).astype(jnp.bfloat16)
    outgoing = jnp.take(proj_grid, grid_send, axis=0)
    arrived = lax.all_to_all(outgoing, "band", split_axis=0, concat_axis=0, tiled=True)
    slot_proj = arrived.reshape(slot_rows, hidden_dev)
    proj_mesh = matmul(mesh_full, w_mesh).astype(jnp.bfloat16)
    enc_pre = jnp.take(slot_proj, enc_source, axis=0).astype(jnp.float32) + jnp.take(
        proj_mesh, enc_target, axis=0
    ).astype(jnp.float32)
    enc_active = jax.nn.silu(enc_pre).astype(jnp.bfloat16)
    enc_table = hot_table(enc_target, mesh_rows)
    enc_summed = inner_rows(enc_table, enc_active).astype(jnp.bfloat16)
    enc_whole = lax.all_gather(enc_summed, "feat", axis=1, tiled=True)
    update = matmul(enc_whole, enc_columns)
    mesh_mid = (mesh_latent.astype(jnp.float32) + update).astype(jnp.bfloat16)
    mid_full = lax.all_gather(mesh_mid, "feat", axis=1, tiled=True)
    proj_send = matmul(mid_full, w_send).astype(jnp.bfloat16)
    proj_recv = matmul(mid_full, w_recv).astype(jnp.bfloat16)
    halo_out = jnp.take(proj_send, mesh_send, axis=0)
    halo_in = lax.all_to_all(halo_out, "band", split_axis=0, concat_axis=0, tiled=True)
    extended = jnp.concatenate([proj_send, halo_in.reshape(halo_rows, hidden_dev)], axis=0)
    proc_pre = jnp.take(extended, proc_source, axis=0).astype(jnp.float32) + jnp.take(
        proj_recv, proc_target, axis=0
    ).astype(jnp.float32)
    proc_active = jax.nn.silu(proc_pre).astype(jnp.bfloat16)
    proc_table = hot_table(proc_target, mesh_rows)
    proc_summed = inner_rows(proc_table, proc_active).astype(jnp.bfloat16)
    proc_whole = lax.all_gather(proc_summed, "feat", axis=1, tiled=True)
    proc_update = matmul(proc_whole, proc_columns)
    mesh_out = (mesh_mid.astype(jnp.float32) + proc_update).astype(jnp.bfloat16)
    cot_full = lax.all_gather(cotangent, "feat", axis=1, tiled=True)
    back_proc = matmul(cot_full, w_proc_out.T).astype(jnp.bfloat16)
    grad_proc_out = inner_rows(proc_summed, cot_full)
    slope_proc = (
        jnp.take(back_proc, proc_target, axis=0).astype(jnp.float32) * silu_slope(proc_pre)
    ).astype(jnp.bfloat16)
    back_recv = inner_rows(proc_table, slope_proc).astype(jnp.bfloat16)
    source_table = hot_table(proc_source, mesh_rows + halo_rows)
    back_ext = inner_rows(source_table, slope_proc).astype(jnp.bfloat16)
    back_halo = back_ext[mesh_rows:].reshape(bands, halo_rows // bands, hidden_dev)
    returned = lax.all_to_all(back_halo, "band", split_axis=0, concat_axis=0, tiled=True)
    returned_sum = jax.ops.segment_sum(
        returned.reshape(halo_rows, hidden_dev).astype(jnp.float32),
        mesh_send.reshape(-1),
        num_segments=mesh_rows,
    )
    back_send = (back_ext[:mesh_rows].astype(jnp.float32) + returned_sum).astype(jnp.bfloat16)
    grad_send = inner_rows(mid_full, back_send)
    grad_recv = inner_rows(mid_full, back_recv)
    send_whole, recv_whole = (
        lax.all_gather(back_send, "feat", axis=1, tiled=True),
        lax.all_gather(back_recv, "feat", axis=1, tiled=True),
    )
    back_sum = matmul(send_whole, send_slice.T) + matmul(recv_whole, recv_slice.T)
    back_mid = (cotangent.astype(jnp.float32) + back_sum).astype(jnp.bfloat16)
    back_full = lax.all_gather(back_mid, "feat", axis=1, tiled=True)
    back_enc = matmul(back_full, w_enc_out.T).astype(jnp.bfloat16)
    grad_enc_out = inner_rows(enc_summed, back_full)
    slope_enc = (
        jnp.take(back_enc, enc_target, axis=0).astype(jnp.float32) * silu_slope(enc_pre)
    ).astype(jnp.bfloat16)
    back_pmesh = inner_rows(enc_table, slope_enc).astype(jnp.bfloat16)
    grad_mesh_w = inner_rows(mesh_full, back_pmesh)
    slot_table = hot_table(enc_source, slot_rows)
    back_slot = inner_rows(slot_table, slope_enc).astype(jnp.bfloat16)
    back_slots = lax.all_to_all(
        back_slot.reshape(bands, slot_rows // bands, hidden_dev),
        "band",
        split_axis=0,
        concat_axis=0,
        tiled=True,
    )
    back_pgrid = jax.ops.segment_sum(
        back_slots.reshape(slot_rows, hidden_dev).astype(jnp.float32),
        grid_send.reshape(-1),
        num_segments=grid_rows,
    ).astype(jnp.bfloat16)
    grad_grid_w = inner_rows(grid_full, back_pgrid)
    pgrid_whole = lax.all_gather(back_pgrid, "feat", axis=1, tiled=True)
    grid_grad = matmul(pgrid_whole, grid_slice.T).astype(jnp.bfloat16)
    grad_grid_w, grad_mesh_w, grad_enc_out, grad_send, grad_recv, grad_proc_out = lax.psum(
        (grad_grid_w, grad_mesh_w, grad_enc_out, grad_send, grad_recv, grad_proc_out), "band"
    )
    return (
        mesh_out,
        grid_grad,
        grad_grid_w * scale,
        grad_mesh_w * scale,
        grad_enc_out * scale,
        grad_send * scale,
        grad_recv * scale,
        grad_proc_out * scale,
    )


def inner_columns(left, right):
    return lax.dot_general(
        left, right, (((1,), (1,)), ((), ())), preferred_element_type=jnp.float32
    )


def hot(condition):
    return jnp.where(condition, 1.0, 0.0).astype(jnp.bfloat16)


def sigmoid(values):
    return 1.0 / (1.0 + jnp.exp(-values))


def fused_kernel(
    bands,
    feats,
    scale,
    grid_latent,
    mesh_latent,
    w_grid_hbm,
    w_mesh_hbm,
    w_enc_hbm,
    w_send_hbm,
    w_recv_hbm,
    w_proc_hbm,
    grid_send_hbm,
    g2m_src,
    g2m_dst,
    mesh_send_hbm,
    m2m_src,
    m2m_dst,
    cotangent,
    mesh_out,
    grid_grad,
    tall_out,
    wide_out,
    w_grid,
    w_mesh,
    w_proc_out,
    grid_send,
    mesh_send,
    index_rows,
    index_columns,
    grid_full,
    mesh_full,
    cot_full,
    enc_full,
    send_full,
    recv_full,
    proc_columns,
    grid_slice,
    grid_pick,
    mesh_pick,
    enc_gather,
    enc_scatter,
    proc_gather,
    proc_scatter,
    enc_rows,
    proc_rows,
    outgoing,
    halo_out,
    enc_pre,
    back_edge,
    edge_values,
    edge_slopes,
    enc_whole,
    mid_full,
    proc_whole,
    recv_whole,
    send_whole,
    back_full,
    back_ext,
    halo_back,
    back_slot,
    slot_back,
    pgrid_whole,
    tall_part,
    tall_land,
    tall_sum,
    wide_part,
    wide_land,
    wide_sum,
    feat_send_sem,
    feat_recv_sem,
    band_send_sem,
    band_recv_sem,
    stage_sem,
):
    band = lax.axis_index("band")
    feat = lax.axis_index("feat")
    width = grid_latent.shape[1]
    rows = mesh_latent.shape[0]
    grid_rows = grid_latent.shape[0]
    slot_peer = grid_send.shape[1]
    halo_peer = mesh_send.shape[1]
    slots = bands * slot_peer
    halos = bands * halo_peer
    edge_rows = g2m_src.shape[0]
    lanes = g2m_src.shape[1]
    ext = rows + halos
    started = []

    def column(place):
        return pl.ds(pl.multiple_of(place * width, width), width)

    def block(place, size):
        return pl.ds(pl.multiple_of(place * size, size), size)

    staged = []

    def stage(source, target):
        copy = pltpu.make_async_copy(source, target, stage_sem.at[len(staged)])
        copy.start()
        staged.append(copy)
        return copy

    index_rows[...] = jnp.zeros_like(index_rows)
    index_copies = [
        stage(source, index_rows.at[pl.ds(place * edge_rows, edge_rows)])
        for place, source in enumerate((g2m_src, g2m_dst, m2m_src, m2m_dst))
    ]
    index_copies += [stage(grid_send_hbm, grid_send), stage(mesh_send_hbm, mesh_send)]
    w_grid_copy = stage(w_grid_hbm, w_grid)
    grid_own = stage(grid_latent, grid_full.at[:, column(feat)])
    mesh_own = stage(mesh_latent, mesh_full.at[:, column(feat)])
    w_mesh_copy = stage(w_mesh_hbm, w_mesh)
    enc_own = stage(w_enc_hbm, enc_full.at[block(feat, width)])
    cot_own = stage(cotangent, cot_full.at[:, column(feat)])
    w_proc_copy = stage(w_proc_hbm, w_proc_out)
    send_own = stage(w_send_hbm, send_full.at[:, column(feat)])
    recv_own = stage(w_recv_hbm, recv_full.at[:, column(feat)])

    barrier = pltpu.get_barrier_semaphore()
    for step in range(1, bands):
        pl.semaphore_signal(
            barrier,
            inc=1,
            device_id={"band": lax.rem(band + step, bands)},
            device_id_type=pl.DeviceIdType.MESH,
        )
    for step in range(1, feats):
        pl.semaphore_signal(
            barrier,
            inc=1,
            device_id={"feat": lax.rem(feat + step, feats)},
            device_id_type=pl.DeviceIdType.MESH,
        )
    pl.semaphore_wait(barrier, bands + feats - 2)

    counts = {"feat": 0, "band": 0}

    def exchange(axis, source, target):
        me, size, send_sem, recv_sem = (
            (feat, feats, feat_send_sem, feat_recv_sem)
            if axis == "feat"
            else (band, bands, band_send_sem, band_recv_sem)
        )
        phase = counts[axis]
        counts[axis] += 1
        copies = []
        for step in range(1, size):
            peer = lax.rem(me + step, size)
            copy = pltpu.make_async_remote_copy(
                src_ref=source(peer),
                dst_ref=target(me),
                send_sem=send_sem.at[phase, step - 1],
                recv_sem=recv_sem.at[phase, step - 1],
                device_id={axis: peer},
                device_id_type=pl.DeviceIdType.MESH,
            )
            copy.start()
            copies.append(copy)
        started.extend(copies)
        return copies

    near = feat + 1 - 2 * lax.rem(feat, 2)
    far = lax.rem(feat + 2, feats)

    def spread(source, place):
        phase = counts["feat"]
        counts["feat"] += 1

        def send(step, part, target, peer):
            copy = pltpu.make_async_remote_copy(
                src_ref=part,
                dst_ref=target,
                send_sem=feat_send_sem.at[phase, step],
                recv_sem=feat_recv_sem.at[phase, step],
                device_id={"feat": peer},
                device_id_type=pl.DeviceIdType.MESH,
            )
            started.append(copy)
            return copy

        across = send(0, source, place(feat), far)
        across.start()
        beside = send(1, source, place(feat), near)
        beside.start()
        onward = send(2, place(far), place(far), near)
        return {"across": across, "beside": beside, "onward": onward, "relayed": False}

    def relay(copies):
        if not copies["relayed"]:
            copies["across"].wait_recv()
            copies["onward"].start()
            copies["relayed"] = True

    def arrive(copies):
        if isinstance(copies, dict):
            relay(copies)
            copies["beside"].wait_recv()
            copies["onward"].wait_recv()
        else:
            for copy in copies:
                copy.wait_recv()

    def gather_columns(source, target):
        return spread(source, lambda owner: target.at[:, column(owner)])

    def gather_held(target):
        return spread(target.at[:, column(feat)], lambda owner: target.at[:, column(owner)])

    grid_copies = gather_columns(grid_latent, grid_full)
    mesh_copies = gather_columns(mesh_latent, mesh_full)

    for copy in index_copies:
        copy.wait()
    index_rows[4 * edge_rows : 4 * edge_rows + bands, 0:slot_peer] = grid_send[...]
    index_rows[4 * edge_rows + bands : 4 * edge_rows + 2 * bands, 0:halo_peer] = mesh_send[...]
    index_columns[...] = index_rows[...].T

    def picks(target, first, size, count):
        place = lax.broadcasted_iota(jnp.int32, (size, count), 1)
        for peer in range(bands):
            chosen = index_columns[0:size, first + peer : first + peer + 1]
            target[peer * size : (peer + 1) * size, :] = hot(chosen == place)

    def edge_gather(target, first, start, count):
        place = lax.broadcasted_iota(jnp.int32, (lanes, count), 1)
        for row in range(edge_rows):
            chosen = index_columns[:, first + row : first + row + 1]
            target[row * lanes : (row + 1) * lanes, start : start + count] = hot(chosen == place)

    def edge_scatter(target, index, start, count):
        place = lax.broadcasted_iota(jnp.int32, (count, lanes), 0)
        for row in range(edge_rows):
            chosen = index_rows[index + row : index + row + 1, :]
            target[start : start + count, row * lanes : (row + 1) * lanes] = hot(chosen == place)

    picks(grid_pick, 4 * edge_rows, slot_peer, grid_rows)

    grid_own.wait()
    w_grid_copy.wait()
    arrive(grid_copies)
    proj_grid = matmul(grid_full[...], w_grid[...]).astype(jnp.bfloat16)
    outgoing[...] = matmul(grid_pick[...], proj_grid).astype(jnp.bfloat16)
    slot_copies = exchange(
        "band",
        lambda peer: outgoing.at[block(peer, slot_peer)],
        lambda me: enc_rows.at[block(me, slot_peer)],
    )
    enc_rows[block(band, slot_peer), :] = outgoing[block(band, slot_peer), :]
    mesh_own.wait()
    w_mesh_copy.wait()
    arrive(mesh_copies)
    enc_weight_copies = spread(w_enc_hbm, lambda owner: enc_full.at[block(owner, width)])
    cot_copies = gather_columns(cotangent, cot_full)
    enc_rows[slots : slots + rows, :] = matmul(mesh_full[...], w_mesh[...]).astype(jnp.bfloat16)
    edge_gather(enc_gather, 0, 0, slots)
    edge_gather(enc_gather, edge_rows, slots, rows)
    edge_scatter(enc_scatter, edge_rows, slots, rows)

    def per_chunk(body):
        size = 2 * lanes

        def step(place, carry):
            body(pl.ds(pl.multiple_of(place * size, size), size))
            return carry

        lax.fori_loop(0, edge_rows // 2, step, 0)

    arrive(slot_copies)

    def enc_forward(edges):
        values = matmul(enc_gather[edges, :], enc_rows[...])
        enc_pre[edges, :] = values
        edge_values[edges, :] = (values * sigmoid(values)).astype(jnp.bfloat16)

    per_chunk(enc_forward)
    enc_summed = matmul(enc_scatter[slots : slots + rows, :], edge_values[...])
    enc_whole[:, column(feat)] = enc_summed.astype(jnp.bfloat16)
    enc_copies = gather_held(enc_whole)
    relay(enc_weight_copies)
    relay(cot_copies)

    def enc_slope(edges):
        enc_pre[edges, :] = silu_slope_of(enc_pre[edges, :])

    per_chunk(enc_slope)
    picks(mesh_pick, 4 * edge_rows + bands, halo_peer, rows)
    edge_gather(proc_gather, 2 * edge_rows, 0, ext)
    edge_gather(proc_gather, 3 * edge_rows, ext, rows)
    enc_own.wait()
    arrive(enc_weight_copies)
    arrive(enc_copies)
    send_own.wait()
    mid_full[...] = (
        mesh_full[...].astype(jnp.float32) + matmul(enc_whole[...], enc_full[...])
    ).astype(jnp.bfloat16)
    proj_send = matmul(mid_full[...], send_full[:, column(feat)]).astype(jnp.bfloat16)
    halo_out[...] = matmul(mesh_pick[...], proj_send).astype(jnp.bfloat16)
    halo_copies = exchange(
        "band",
        lambda peer: halo_out.at[block(peer, halo_peer)],
        lambda me: proc_rows.at[pl.ds(pl.multiple_of(rows + me * halo_peer, halo_peer), halo_peer)],
    )
    send_weight_copies = gather_columns(w_send_hbm, send_full)
    recv_weight_copies = gather_columns(w_recv_hbm, recv_full)
    recv_own.wait()
    proc_rows[pl.ds(pl.multiple_of(rows + band * halo_peer, halo_peer), halo_peer), :] = halo_out[
        block(band, halo_peer), :
    ]
    proc_rows[0:rows, :] = proj_send
    proc_rows[ext : ext + rows, :] = matmul(mid_full[...], recv_full[:, column(feat)]).astype(jnp.bfloat16)
    cot_own.wait()
    w_proc_copy.wait()
    arrive(cot_copies)
    back_proc = inner_columns(cot_full[...], w_proc_out[...]).astype(jnp.bfloat16)
    back_edge[...] = matmul(proc_gather[:, ext : ext + rows], back_proc)
    edge_scatter(proc_scatter, 2 * edge_rows, 0, ext)
    edge_scatter(proc_scatter, 3 * edge_rows, ext, rows)
    arrive(halo_copies)

    def proc_forward(edges):
        values = matmul(proc_gather[edges, :], proc_rows[...])
        sigma = sigmoid(values)
        edge_values[edges, :] = (values * sigma).astype(jnp.bfloat16)
        slope = sigma * (1.0 + values * (1.0 - sigma))
        edge_slopes[edges, :] = (back_edge[edges, :] * slope).astype(jnp.bfloat16)

    per_chunk(proc_forward)
    back_ext[...] = matmul(proc_scatter[...], edge_slopes[...]).astype(jnp.bfloat16)
    halo_back_copies = exchange(
        "band",
        lambda peer: back_ext.at[pl.ds(pl.multiple_of(rows + peer * halo_peer, halo_peer), halo_peer)],
        lambda me: halo_back.at[block(me, halo_peer)],
    )
    halo_back[block(band, halo_peer), :] = back_ext[
        pl.ds(pl.multiple_of(rows + band * halo_peer, halo_peer), halo_peer), :
    ]
    recv_whole[:, column(feat)] = back_ext[ext : ext + rows, :]
    recv_copies = gather_held(recv_whole)
    relay(send_weight_copies)
    relay(recv_weight_copies)
    proc_summed = matmul(proc_scatter[ext : ext + rows, :], edge_values[...]).astype(jnp.bfloat16)
    proc_whole[:, column(feat)] = proc_summed

    tall = tall_part.shape[1] // bands
    wide = wide_part.shape[1] // bands

    def scatter_sum(part, land, place, size, value):
        part[place] = value.astype(jnp.bfloat16)
        return exchange(
            "band",
            lambda peer: part.at[place, block(peer, size)],
            lambda me: land.at[place, me],
        )

    def add_up(copies, part, land, total, place, size):
        arrive(copies)
        mine = part[place, block(band, size), :]
        land[place, band] = mine
        value = land[place, 0].astype(jnp.float32)
        for other in range(1, bands):
            value = value + land[place, other].astype(jnp.float32)
        total[place, block(band, size), :] = (value * scale).astype(jnp.bfloat16)
        held = total.at[place, block(band, size)]
        return exchange("band", lambda peer: held, lambda me: held)

    grad_proc = scatter_sum(
        wide_part, wide_land, 0, wide, inner_rows(proc_summed, cot_full[...])
    )
    edge_scatter(enc_scatter, 0, 0, slots)
    relay(recv_copies)
    arrive(halo_back_copies)
    back_send = (
        back_ext[0:rows, :].astype(jnp.float32) + inner_rows(mesh_pick[...], halo_back[...])
    ).astype(jnp.bfloat16)
    send_whole[:, column(feat)] = back_send
    send_copies = gather_held(send_whole)
    proc_copies = gather_held(proc_whole)
    column_copies = exchange(
        "feat",
        lambda peer: w_proc_out.at[:, column(peer)],
        lambda me: proc_columns.at[block(me, width)],
    )
    proc_columns[block(feat, width), :] = w_proc_out[:, column(feat)]
    slice_copies = exchange(
        "feat",
        lambda peer: w_grid.at[block(peer, width)],
        lambda me: grid_slice.at[:, column(me)],
    )
    grid_slice[:, column(feat)] = w_grid[block(feat, width), :]
    grad_send = scatter_sum(tall_part, tall_land, 0, tall, inner_rows(mid_full[...], back_send))
    grad_recv = scatter_sum(
        tall_part, tall_land, 1, tall, inner_rows(mid_full[...], back_ext[ext : ext + rows, :])
    )
    arrive(send_weight_copies)
    arrive(recv_weight_copies)
    arrive(recv_copies)
    back_sum = cot_full[...].astype(jnp.float32) + inner_columns(recv_whole[...], recv_full[...])
    relay(send_copies)
    proc_total = add_up(grad_proc, wide_part, wide_land, wide_sum, 0, wide)
    arrive(send_copies)
    back_full[...] = (back_sum + inner_columns(send_whole[...], send_full[...])).astype(
        jnp.bfloat16
    )
    back_enc = inner_columns(back_full[...], enc_full[block(feat, width), :]).astype(jnp.bfloat16)
    back_edge[...] = matmul(enc_gather[:, slots : slots + rows], back_enc)

    def enc_backward(edges):
        edge_slopes[edges, :] = (back_edge[edges, :] * enc_pre[edges, :]).astype(jnp.bfloat16)

    per_chunk(enc_backward)
    back_slot[...] = matmul(enc_scatter[...], edge_slopes[...]).astype(jnp.bfloat16)
    slot_back_copies = exchange(
        "band",
        lambda peer: back_slot.at[block(peer, slot_peer)],
        lambda me: slot_back.at[block(me, slot_peer)],
    )
    slot_back[block(band, slot_peer), :] = back_slot[block(band, slot_peer), :]
    grad_mesh = scatter_sum(
        tall_part,
        tall_land,
        2,
        tall,
        inner_rows(mesh_full[...], back_slot[slots : slots + rows, :]),
    )
    grad_enc = scatter_sum(
        wide_part, wide_land, 1, wide, inner_rows(enc_whole[:, column(feat)], back_full[...])
    )
    send_total = add_up(grad_send, tall_part, tall_land, tall_sum, 0, tall)
    recv_total = add_up(grad_recv, tall_part, tall_land, tall_sum, 1, tall)
    arrive(slot_back_copies)
    back_pgrid = inner_rows(grid_pick[...], slot_back[...]).astype(jnp.bfloat16)
    pgrid_whole[:, column(feat)] = back_pgrid
    grad_grid = scatter_sum(
        tall_part, tall_land, 3, tall, inner_rows(grid_full[...], back_pgrid)
    )
    pgrid_copies = gather_held(pgrid_whole)
    mesh_total = add_up(grad_mesh, tall_part, tall_land, tall_sum, 2, tall)
    enc_total = add_up(grad_enc, wide_part, wide_land, wide_sum, 1, wide)
    grid_total = add_up(grad_grid, tall_part, tall_land, tall_sum, 3, tall)
    arrive(proc_copies)
    arrive(column_copies)
    mesh_out[...] = (
        mid_full[:, column(feat)].astype(jnp.float32)
        + matmul(proc_whole[...], proc_columns[...])
    ).astype(jnp.bfloat16)
    arrive(slice_copies)
    arrive(pgrid_copies)
    grid_grad[...] = inner_columns(pgrid_whole[...], grid_slice[...]).astype(jnp.bfloat16)
    for total in (proc_total, send_total, recv_total, mesh_total, enc_total, grid_total):
        arrive(total)
    tall_out[...] = tall_sum[...]
    wide_out[...] = wide_sum[...]
    for copy in started:
        copy.wait_send()


def write_kernel(
    mesh_held,
    grid_held,
    tall_hbm,
    wide_hbm,
    mesh_out,
    grid_grad,
    out_grid,
    out_mesh,
    out_enc,
    out_send,
    out_recv,
    out_proc,
    tall_held,
    wide_held,
    tall_wide,
    wide_wide,
    copy_sem,
    load_sem,
):
    loads = [
        pltpu.make_async_copy(tall_hbm, tall_held, load_sem.at[0]),
        pltpu.make_async_copy(wide_hbm, wide_held, load_sem.at[1]),
    ]
    for load in loads:
        load.start()
    copies = [
        pltpu.make_async_copy(mesh_held, mesh_out, copy_sem.at[0]),
        pltpu.make_async_copy(grid_held, grid_grad, copy_sem.at[1]),
    ]
    for copy in copies:
        copy.start()
    for load in loads:
        load.wait()
    for held, wide, place, target in (
        (tall_held, tall_wide, 0, out_send),
        (tall_held, tall_wide, 1, out_recv),
        (tall_held, tall_wide, 2, out_mesh),
        (tall_held, tall_wide, 3, out_grid),
        (wide_held, wide_wide, 0, out_proc),
        (wide_held, wide_wide, 1, out_enc),
    ):
        wide[place] = held[place].astype(jnp.float32)
        copy = pltpu.make_async_copy(wide.at[place], target, copy_sem.at[len(copies)])
        copy.start()
        copies.append(copy)
    for copy in copies:
        copy.wait()


def silu_slope_of(values):
    sigma = sigmoid(values)
    return sigma * (1.0 + values * (1.0 - sigma))


def per_device(*arrays):
    (grid_latent, mesh_latent, w_grid, _, w_enc_out) = arrays[:5]
    grid_send, g2m_src, mesh_send = arrays[8], arrays[9], arrays[11]
    bands = lax.axis_size("band")
    feats = lax.axis_size("feat")
    slot_peer, halo_peer = grid_send.shape[1], mesh_send.shape[1]
    rows, width = mesh_latent.shape
    grid_rows = grid_latent.shape[0]
    latent = w_grid.shape[0]
    edge_rows, lanes = g2m_src.shape
    if feats != 4 or edge_rows % 8 or slot_peer % 16 or halo_peer % 16 or width % (16 * bands) or 4 * edge_rows + 2 * bands > lanes:
        return per_device_collectives(*arrays)
    slots, halos = bands * slot_peer, bands * halo_peer
    ext = rows + halos
    edges = edge_rows * lanes
    scale = 1.0 / math.sqrt(rows * bands)

    def half(*shape):
        return pltpu.VMEM(shape, jnp.bfloat16)

    def full(*shape):
        return pltpu.VMEM(shape, jnp.float32)

    feat_phases, band_phases = 13, 16
    scratch = [
        half(latent, width),
        half(latent, width),
        half(width, latent),
        pltpu.VMEM(grid_send.shape, jnp.int32),
        pltpu.VMEM(mesh_send.shape, jnp.int32),
        pltpu.VMEM((lanes, lanes), jnp.int32),
        pltpu.VMEM((lanes, lanes), jnp.int32),
        half(grid_rows, latent),
        half(rows, latent),
        half(rows, latent),
        half(latent, latent),
        half(latent, latent),
        half(latent, latent),
        half(latent, width),
        half(width, latent),
        half(slots, grid_rows),
        half(halos, rows),
        half(edges, slots + rows),
        half(slots + rows, edges),
        half(edges, ext + rows),
        half(ext + rows, edges),
        half(slots + rows, width),
        half(ext + rows, width),
        half(slots, width),
        half(halos, width),
        full(edges, width),
        full(edges, width),
        half(edges, width),
        half(edges, width),
        half(rows, latent),
        half(rows, latent),
        half(rows, latent),
        half(rows, latent),
        half(rows, latent),
        half(rows, latent),
        half(ext + rows, width),
        half(halos, width),
        half(slots + rows, width),
        half(slots, width),
        half(grid_rows, latent),
        half(4, latent, width),
        half(4, bands, latent // bands, width),
        half(4, latent, width),
        half(2, width, latent),
        half(2, bands, width // bands, latent),
        half(2, width, latent),
        pltpu.SemaphoreType.DMA((feat_phases, feats - 1)),
        pltpu.SemaphoreType.DMA((feat_phases, feats - 1)),
        pltpu.SemaphoreType.DMA((band_phases, bands - 1)),
        pltpu.SemaphoreType.DMA((band_phases, bands - 1)),
        pltpu.SemaphoreType.DMA((len(arrays),)),
    ]
    tall = jax.ShapeDtypeStruct((latent, width), jnp.float32)
    wide = jax.ShapeDtypeStruct((width, latent), jnp.float32)
    nodes = (
        jax.ShapeDtypeStruct((rows, width), jnp.bfloat16),
        jax.ShapeDtypeStruct((grid_rows, width), jnp.bfloat16),
    )
    sums = (
        jax.ShapeDtypeStruct((4, latent, width), jnp.bfloat16),
        jax.ShapeDtypeStruct((2, width, latent), jnp.bfloat16),
    )
    vmem = pl.BlockSpec(memory_space=pltpu.VMEM)
    hbm = pl.BlockSpec(memory_space=pltpu.HBM)
    held = pl.pallas_call(
        functools.partial(fused_kernel, bands, feats, scale),
        out_shape=nodes + sums,
        in_specs=[hbm] * len(arrays),
        out_specs=(vmem,) * 4,
        scratch_shapes=scratch,
        compiler_params=pltpu.CompilerParams(
            collective_id=0, has_side_effects=True, vmem_limit_bytes=61 * 1024 * 1024
        ),
    )(*arrays)
    return pl.pallas_call(
        write_kernel,
        out_shape=nodes + (tall, tall, wide, tall, tall, wide),
        in_specs=[hbm] * 4,
        out_specs=(hbm,) * 8,
        scratch_shapes=[
            half(4, latent, width),
            half(2, width, latent),
            full(4, latent, width),
            full(2, width, latent),
            pltpu.SemaphoreType.DMA((8,)),
            pltpu.SemaphoreType.DMA((2,)),
        ],
        compiler_params=pltpu.CompilerParams(vmem_limit_bytes=61 * 1024 * 1024),
    )(*held)


def solution(mesh):
    in_specs = (
        P("band", "feat"),
        P("band", "feat"),
        P(None, "feat"),
        P(None, "feat"),
        P("feat", None),
        P(None, "feat"),
        P(None, "feat"),
        P("feat", None),
        P("band", None),
        P("band", None),
        P("band", None),
        P("band", None),
        P("band", None),
        P("band", None),
        P("band", "feat"),
    )
    out_specs = (
        P("band", "feat"),
        P("band", "feat"),
        P(None, "feat"),
        P(None, "feat"),
        P("feat", None),
        P(None, "feat"),
        P(None, "feat"),
        P("feat", None),
    )
    return jax.shard_map(
        per_device, mesh=mesh, in_specs=in_specs, out_specs=out_specs, check_vma=False
    )
```
